32 devices in a mesh: img: 4 (over y, x), row: 4 (over z), col: 2 (over core).
Axes of the slice: x: 2, y: 2, z: 4, core: 2. Of those that a mesh axis runs over, the one named last changes fastest.
Arguments:
- features: bfloat16 [4, 96, 64, 2048], P('img', 'row', 'col'), may hold values from -6 to 6
- region_boxes: int32 [4, 8, 4], P('img'), may hold values from 0 to 96, as said below
- labels: int32 [4, 96, 64], P('img', 'row', 'col'), may hold values from 0 to 149
- branch_projection_weight: bfloat16 [4, 2048, 512], replicated, may hold values from -0.125 to 0.125
- branch_gain: float32 [4, 512], replicated, may hold values from 0.5 to 1.5
- branch_bias: float32 [4, 512], replicated, may hold values from -3 to 3
- conv_w: bfloat16 [4096, 9, 512], P(('row', 'col')), may hold values from -0.03125 to 0.03125
- conv_gain: float32 [512], replicated, may hold values from 0.5 to 1.5
- conv_bias: float32 [512], replicated, may hold values from -3 to 3
- class_w: bfloat16 [512, 150], replicated, may hold values from -0.75 to 0.75
- class_bias: float32 [150], replicated, may hold values from -4 to 4
Outputs:
- logits: float32 [4, 96, 64, 150], P('img', 'row', 'col')
- feature_grad: float32 [4, 96, 64, 2048], P('img', 'row', 'col')
- branch_w_grad: float32 [4, 2048, 512], P(None, ('row', 'col'))
- branch_gain_grad: float32 [4, 512], replicated
- branch_bias_grad: float32 [4, 512], replicated
- conv_w_grad: float32 [4096, 9, 512], P(('row', 'col'))
- conv_gain_grad: float32 [512], replicated
- conv_bias_grad: float32 [512], replicated
- class_w_grad: float32 [512, 150], replicated
- class_bias_grad: float32 [150], replicated
The draws below stay inside these ranges and needn't reach their ends.
Inputs may be any that keep to these rules, and one draw needn't show every extreme that they name: `region_boxes`: in every canvas the 8 boxes (y0, x0, y1, x1, ends excluded) tile the 96 x 64 canvas exactly; each is at least 2 cells high and 2 wide.
All inputs are finite; a program needn't handle non-finite values.
Results may differ from the reference program's by a relative error of at most 0.012.
Values may be sent and summed in bfloat16 or wider, within the bound.
No kernel may reach another device: no remote copies, remote signals or barrier semaphores. Data moves between devices by JAX's collectives and lax.ppermute only.
A program may use at most 448 MiB of HBM per device.

```python
from functools import partial
import jax
import jax.numpy as jnp
from jax import lax

TILE_H = 24
TILE_W = 32
CIN = 2048
BR = 512
MID = 512
CLS = 150
CAT = 4096
CANVASES = 4
HEIGHT = 96
WIDTH = 64


def canvas_layout(key):
    parts = jax.random.split(key, 5)
    strip = jax.random.randint(parts[0], (), 2, TILE_W - 1)
    band = jax.random.randint(parts[1], (), 2, TILE_H + 1)
    rest_h = HEIGHT - band
    jitter_y = rest_h // 4 - 1
    middle_y = band + rest_h // 2 + jax.random.randint(parts[2], (), -jitter_y, jitter_y + 1)
    rest_w = WIDTH - strip
    jitter_x = rest_w // 12
    first_cut = strip + rest_w // 3 + jax.random.randint(parts[3], (), -jitter_x, jitter_x + 1)
    second_cut = strip + 2 * rest_w // 3 + jax.random.randint(parts[4], (), -jitter_x, jitter_x + 1)
    zero = jnp.zeros((), jnp.int32)
    full_h = jnp.full((), HEIGHT, jnp.int32)
    full_w = jnp.full((), WIDTH, jnp.int32)
    boxes_list = [jnp.stack([zero, zero, full_h, strip]), jnp.stack([zero, strip, band, full_w])]
    for upper, lower in ((band, middle_y), (middle_y, full_h)):
        for leftmost, rightmost in ((strip, first_cut), (first_cut, second_cut), (second_cut, full_w)):
            boxes_list.append(jnp.stack([upper, leftmost, lower, rightmost]))
    return jnp.stack(boxes_list).astype(jnp.int32)


def draw_region_boxes(key, part):
    keys = jax.random.split(jax.random.fold_in(key, 17), CANVASES)
    return jax.vmap(canvas_layout)(keys)


def touch_ends(result, own_key, smallest, top_value):
    longest = result.shape.index(max(result.shape))
    spots = []
    for shift in (0, 1):
        where = [jax.random.randint(jax.random.fold_in(own_key, axis), (), 0, length) for axis, length in enumerate(result.shape)]
        where[longest] = (where[longest] + shift) % result.shape[longest]
        spots.append(tuple(where))
    return result.at[spots[0]].set(smallest).at[spots[1]].set(top_value)


def block_levels(stream_key, dims, cuts, smallest, largest):
    loudness, own = 1.0, jax.random.fold_in(stream_key, 6)
    for axis_at, blocks in cuts:
        steps = jnp.exp(jax.random.uniform(jax.random.fold_in(own, axis_at), (blocks,), jnp.float32, smallest / len(cuts), largest / len(cuts)))
        loudness = loudness * jnp.repeat(steps, dims[axis_at] // blocks).reshape([-1 if axis == axis_at else 1 for axis in range(len(dims))])
    return loudness


def bell_draw(stream_key, shape, scale, limit, cuts=(), kind=jnp.bfloat16):
    values = jax.random.normal(stream_key, shape, jnp.float32) * scale
    if len(cuts) > 0:
        values = block_levels(stream_key, shape, cuts, -0.22, 0.18) * values
    return jnp.clip(values, min=-limit, max=limit).astype(kind)


def setup_inputs(seed: int = 0) -> dict:
    key_list = jax.random.split(jax.random.key(seed), 12)
    features = bell_draw(key_list[0], (CANVASES, HEIGHT, WIDTH, CIN), 1.0, 6.0, ((0, 4), (1, 4), (2, 2)))
    region_boxes = draw_region_boxes(jax.random.fold_in(key_list[11], 71), 0)
    labels = touch_ends(jax.random.randint(key_list[2], (CANVASES, HEIGHT, WIDTH), 0, CLS), jax.random.fold_in(key_list[2], 1), 0, CLS - 1).astype(jnp.int32)
    branch_projection_weight = bell_draw(key_list[3], (4, CIN, BR), CIN ** -0.5, 0.125)
    branch_gain = jnp.clip(jax.random.uniform(key_list[4], (4, BR), jnp.float32, 0.5, 1.5), 0.5, 1.5)
    branch_bias = bell_draw(key_list[5], (4, BR), 0.5, 3.0, (), jnp.float32)
    conv_w = bell_draw(key_list[6], (CAT, 9, MID), (9 * CAT) ** -0.5, 0.03125, ((0, 8),))
    conv_gain = jnp.clip(jax.random.uniform(key_list[7], (MID,), jnp.float32, 0.5, 1.5), 0.5, 1.5)
    conv_bias = bell_draw(key_list[8], (MID,), 0.5, 3.0, (), jnp.float32)
    class_w = bell_draw(key_list[9], (MID, CLS), (MID // 8) ** -0.5, 0.75)
    class_bias = bell_draw(key_list[10], (CLS,), 1.0, 4.0, (), jnp.float32)
    return dict(features=features, region_boxes=region_boxes, labels=labels, branch_projection_weight=branch_projection_weight, branch_gain=branch_gain, branch_bias=branch_bias, conv_w=conv_w, conv_gain=conv_gain, conv_bias=conv_bias, class_w=class_w, class_bias=class_bias)


bin_scales = (1, 2, 3, 6)
norm_eps = 1e-05
highest_precision = lax.Precision.HIGHEST
tap_offsets = ((-1, -1), (-1, 0), (-1, 1), (0, -1), (0, 0), (0, 1), (1, -1), (1, 0), (1, 1))

@jax.custom_vjp
def low(v):
    return lax.optimization_barrier(v.astype(jnp.bfloat16)).astype(jnp.float32)

@jax.custom_vjp
def lower_backward(v):
    return v

def low_keep(v):
    return (low(v), None)

def low_pass(kept, grad):
    return (grad,)

def back_keep(v):
    return (v, None)

def back_low(kept, grad):
    return (low(grad),)
low.defvjp(low_keep, low_pass)
lower_backward.defvjp(back_keep, back_low)

def region_index(canvas_box, row_cells, col_cells):
    upper = canvas_box[:, 0][:, None, None]
    leftmost = canvas_box[:, 1][:, None, None]
    lower = canvas_box[:, 2][:, None, None]
    rightmost = canvas_box[:, 3][:, None, None]
    inside = (row_cells[None, :, None] >= upper) & (row_cells[None, :, None] < lower)
    inside = inside & (col_cells[None, None, :] >= leftmost) & (col_cells[None, None, :] < rightmost)
    number = jnp.arange(1, canvas_box.shape[0] + 1, dtype=jnp.int32)[:, None, None]
    return lax.optimization_barrier(jnp.sum(inside.astype(jnp.int32) * number, axis=0)) - 1

def axis_tables(first, last, cells, bin_scale):
    extent = last - first
    across = jnp.arange(bin_scale, dtype=jnp.int32)
    lo_edge = first[:, None] + across[None, :] * extent[:, None] // bin_scale
    hi_edge = first[:, None] + ((across[None, :] + 1) * extent[:, None] + bin_scale - 1) // bin_scale
    member = ((cells[None, None, :] >= lo_edge[:, :, None]) & (cells[None, None, :] < hi_edge[:, :, None])).astype(jnp.float32)
    numer = (cells[None, :] - first[:, None]) * (bin_scale - 1)
    denom = extent[:, None] - 1
    lower_bin = numer // denom
    fraction = (numer - lower_bin * denom).astype(jnp.float32) / denom.astype(jnp.float32)
    upper_bin = jnp.minimum(lower_bin + 1, bin_scale - 1)
    inside = ((cells[None, :] >= first[:, None]) & (cells[None, :] < last[:, None])).astype(jnp.float32)
    weight = (across[None, :, None] == lower_bin[:, None, :]).astype(jnp.float32) * (1.0 - fraction)[:, None, :]
    weight = weight + (across[None, :, None] == upper_bin[:, None, :]).astype(jnp.float32) * fraction[:, None, :]
    weight = weight * inside[:, None, :]
    return (member, (hi_edge - lo_edge).astype(jnp.float32), weight)

def bin_tables(canvas_box, row_cells, col_cells, bin_scale):
    member_y, size_y, weight_y = axis_tables(canvas_box[:, 0], canvas_box[:, 2], row_cells, bin_scale)
    member_x, size_x, weight_x = axis_tables(canvas_box[:, 1], canvas_box[:, 3], col_cells, bin_scale)
    bins = canvas_box.shape[0] * bin_scale * bin_scale
    cells = row_cells.shape[0] * col_cells.shape[0]
    average_pooling = (member_y[:, :, None, :, None] * member_x[:, None, :, None, :]).reshape(bins, cells)
    sizes = (size_y[:, :, None] * size_x[:, None, :]).reshape(bins)
    spread = (weight_y[:, :, None, :, None] * weight_x[:, None, :, None, :]).reshape(bins, cells)
    return (average_pooling, sizes, spread)

def forward(feat, branch_projection_weight, branch_gain, branch_bias, conv_w, conv_gain, conv_bias, class_w, class_bias, region_boxes, labels):
    canvases = feat.shape[0]
    row_cells = jnp.arange(HEIGHT, dtype=jnp.int32)
    col_cells = jnp.arange(WIDTH, dtype=jnp.int32)
    flattened_values = feat.reshape(canvases, HEIGHT * WIDTH, CIN)
    channels = [flattened_values]
    for branch_position, bin_scale in enumerate(bin_scales):
        average_pooling, sizes, spread = jax.vmap(partial(bin_tables, row_cells=row_cells, col_cells=col_cells, bin_scale=bin_scale))(region_boxes)
        region_sum_values = jnp.einsum('owi,oix->owx', average_pooling, flattened_values, precision=highest_precision)
        pooled_features = low(region_sum_values / sizes[:, :, None])
        branch_preactivation = lower_backward(jnp.einsum('sza,aj->szj', pooled_features, branch_projection_weight[branch_position], precision=highest_precision))
        center = lax.optimization_barrier(jnp.mean(branch_preactivation, axis=(0, 1)))
        variance = lax.optimization_barrier(jnp.mean(branch_preactivation * branch_preactivation, axis=(0, 1))) - center * center
        normed = (branch_preactivation - center) * lax.rsqrt(variance + norm_eps)
        activ = jax.nn.silu(branch_gain[branch_position] * normed + branch_bias[branch_position])
        upsampled = jnp.einsum('cbp,cbo->cpo', spread, activ, precision=highest_precision)
        channels.append(low(upsampled))
    joined = jnp.concatenate(channels, axis=-1).reshape(canvases, HEIGHT, WIDTH, CAT)
    product = jnp.einsum('chwi,itm->chwtm', joined, conv_w, precision=highest_precision)
    padded = jnp.pad(product, ((0, 0), (1, 1), (1, 1), (0, 0), (0, 0)))
    region = jax.vmap(partial(region_index, row_cells=row_cells, col_cells=col_cells))(region_boxes)
    region_pad = jnp.pad(region, ((0, 0), (1, 1), (1, 1)), constant_values=-1)
    hidden = jnp.zeros((canvases, HEIGHT, WIDTH, MID), jnp.float32)
    for tap_index, (shift_y, shift_x) in enumerate(tap_offsets):
        window = padded[:, 1 + shift_y:1 + shift_y + HEIGHT, 1 + shift_x:1 + shift_x + WIDTH, tap_index]
        same = (region_pad[:, 1 + shift_y:1 + shift_y + HEIGHT, 1 + shift_x:1 + shift_x + WIDTH] == region).astype(jnp.float32)
        hidden = hidden + same[..., None] * window
    hidden = lower_backward(hidden)
    center = lax.optimization_barrier(jnp.mean(hidden, axis=(0, 1, 2)))
    variance = lax.optimization_barrier(jnp.mean(hidden * hidden, axis=(0, 1, 2))) - center * center
    normed = (hidden - center) * lax.rsqrt(variance + norm_eps)
    act = low(jax.nn.silu(conv_gain * normed + conv_bias))
    logits = lower_backward(jnp.einsum('chwm,mk->chwk', act, class_w, precision=highest_precision) + class_bias)
    onehot = (labels[..., None] == jnp.arange(CLS, dtype=jnp.int32)).astype(jnp.float32)
    loss = jnp.sum(jax.nn.logsumexp(logits, axis=-1) - lax.optimization_barrier(jnp.sum(logits * onehot, axis=-1)))
    return (loss, logits)

def reference(features, region_boxes, labels, branch_projection_weight, branch_gain, branch_bias, conv_w, conv_gain, conv_bias, class_w, class_bias):
    floats = (features.astype(jnp.float32), branch_projection_weight.astype(jnp.float32), branch_gain, branch_bias, conv_w.astype(jnp.float32), conv_gain, conv_bias, class_w.astype(jnp.float32), class_bias)

    def closed(*params):
        return forward(*params, region_boxes, labels)
    loss, pullback, logits = jax.vjp(closed, *floats, has_aux=True)
    grads = pullback(jnp.ones((), jnp.float32))
    return (logits, grads[0], grads[1], grads[2], grads[3], grads[4], grads[5], grads[6], grads[7], grads[8])
```

```python
import jax
import jax.numpy as jnp
import numpy as np
from jax import lax
from jax.experimental import pallas as pl
from jax.experimental.pallas import tpu as pltpu
from jax.sharding import PartitionSpec as P

bin_scales = (1, 2, 3, 6)
norm_eps = 1e-05
tap_offsets = ((-1, -1), (-1, 0), (-1, 1), (0, -1), (0, 0), (0, 1), (1, -1), (1, 0), (1, 1))
contract_first = (((0,), (0,)), ((), ()))
contract_last = (((1,), (1,)), ((), ()))
bf16 = jnp.bfloat16
f32 = jnp.float32


def dot(a, b, dims=(((1,), (0,)), ((), ()))):
    return lax.dot_general(a, b, dims, preferred_element_type=f32)


def swap(value, axis, step):
    count = lax.axis_size(axis)
    return lax.ppermute(value, axis, [(i, i ^ step) for i in range(count)])


def butterfly(value, axes):
    for axis in axes:
        step = 1
        while step < lax.axis_size(axis):
            value = value + swap(value, axis, step)
            step *= 2
    return value


def bin_constants(regions):
    rows = []
    for position, scale in enumerate(bin_scales):
        for r in range(regions):
            for i in range(scale):
                for j in range(scale):
                    rows.append((position, scale, r, i, j))
    return np.asarray(rows, np.int32)


def of_bin_boxes(canvas_box, table):
    pick = jnp.asarray(table[:, 2:3] == np.arange(canvas_box.shape[0])[None, :], jnp.int32)
    return jnp.sum(pick[:, :, None] * canvas_box[None], axis=1)


def members(edges, cells_y, cells_x):
    lo_y, hi_y, lo_x, hi_x = (edge[:, None] for edge in edges)
    y, x = cells_y[None, :], cells_x[None, :]
    return ((y >= lo_y) & (y < hi_y) & (x >= lo_x) & (x < hi_x)).astype(bf16)


def axis_weight(cells, first, last, scale, index):
    extent = (last - first - 1).astype(f32)[:, None]
    place = ((cells[None, :] - first[:, None]) * (scale - 1)[:, None]).astype(f32)
    away = jnp.abs(place - index.astype(f32)[:, None] * extent) / extent
    inside = (cells[None, :] >= first[:, None]) & (cells[None, :] < last[:, None])
    return jnp.where(inside, jnp.maximum(1.0 - away, 0.0), 0.0)


def spreads(boxes, table, cells_y, cells_x):
    scale, i, j = (jnp.asarray(table[:, k]) for k in (1, 3, 4))
    weight_y = axis_weight(cells_y, boxes[:, 0], boxes[:, 2], scale, i)
    weight_x = axis_weight(cells_x, boxes[:, 1], boxes[:, 3], scale, j)
    return (weight_y * weight_x).astype(bf16)


def grid_cells(rows, cols):
    y = jnp.broadcast_to(rows[:, None], (rows.shape[0], cols.shape[0])).reshape(-1)
    x = jnp.broadcast_to(cols[None, :], (rows.shape[0], cols.shape[0])).reshape(-1)
    return y, x


def row_masks(canvas_box, rows, cols):
    y, x = rows[:, None], cols[None, :]
    up, left, down, right = (canvas_box[:, k][:, None, None] for k in range(4))
    inside = (y >= up) & (y < down) & (x >= left) & (x < right)
    upper = jnp.any(inside & (y > up), axis=0)
    lower = jnp.any(inside & (y + 1 < down), axis=0)
    return upper.reshape(-1), lower.reshape(-1)


def shift_lines(box_ref, first, x_ref, o_ref, width, reverse):
    cells, block = x_ref.shape
    order = (2, 1, 0) if reverse else (0, 1, 2)
    left_at, mid_at, right_at = (place * block for place in order)

    def line(at, carry):
        y = first + at
        here = pl.ds(pl.multiple_of(at * width, width), width)
        x = lax.broadcasted_iota(jnp.int32, (width, block), 0)
        no_left = x == 0
        no_right = x == width - 1
        for r in range(box_ref.shape[0]):
            inside = (y >= box_ref[r, 0]) & (y < box_ref[r, 2])
            no_left = no_left | (x == jnp.where(inside, box_ref[r, 1], -1))
            no_right = no_right | (x == jnp.where(inside, box_ref[r, 3] - 1, -1))
        own = x_ref[here, :]
        wide = own.astype(f32)
        left = jnp.where(no_left, 0.0, pltpu.roll(wide, 1, 0))
        right = jnp.where(no_right, 0.0, pltpu.roll(wide, width - 1, 0))
        o_ref[here, left_at : left_at + block] = left.astype(bf16)
        o_ref[here, mid_at : mid_at + block] = own
        o_ref[here, right_at : right_at + block] = right.astype(bf16)
        return carry

    lax.fori_loop(0, cells // width, line, 0)


def shifted(x, canvas_box, first_line, width, reverse=False, places=None, out_blocks=1, into=None):
    blocks, cells, block = x.shape
    total = cells // width
    lines = max(k for k in range(1, total + 1) if total % k == 0 and k * width <= 2048)
    if places is None:
        places, out_blocks = jnp.arange(blocks, dtype=jnp.int32), blocks

    def body(place_ref, first_ref, box_ref, x_ref, *rest):
        first = first_ref[0] + pl.program_id(1) * lines
        shift_lines(box_ref, first, x_ref.at[0], rest[-1].at[0], width, reverse)

    extra = [] if into is None else [into]
    return pl.pallas_call(
        body,
        grid_spec=pltpu.PrefetchScalarGridSpec(
            num_scalar_prefetch=2,
            grid=(blocks, total // lines),
            in_specs=[
                pl.BlockSpec(memory_space=pltpu.SMEM),
                pl.BlockSpec((1, width * lines, block), lambda b, i, at, first: (b, i, 0)),
            ]
            + [pl.BlockSpec(memory_space=pl.ANY)] * len(extra),
            out_specs=pl.BlockSpec(
                (1, width * lines, 3 * block), lambda b, i, at, first: (at[b], i, 0)
            ),
        ),
        out_shape=jax.ShapeDtypeStruct((out_blocks, cells, 3 * block), bf16),
        input_output_aliases={4: 0} if extra else {},
        compiler_params=pltpu.CompilerParams(vmem_limit_bytes=40 << 20),
        cost_estimate=pl.CostEstimate(
            flops=0, bytes_accessed=8 * blocks * cells * block, transcendentals=0
        ),
    )(places, jnp.reshape(first_line, (1,)).astype(jnp.int32), canvas_box, x, *extra)


def silu_slope(value):
    sigmoid_value = jax.nn.sigmoid(value)
    return sigmoid_value * (1.0 + value * (1.0 - sigmoid_value))


def choose(options, index):
    value = options[0]
    for k in range(1, len(options)):
        value = jnp.where(index == k, options[k], value)
    return value


def table_at(values, index):
    return choose([jnp.int32(value) for value in values], index)


def tie(*arrays):
    return list(lax.optimization_barrier(tuple(arrays)))


class Rows:
    def __init__(self, own):
        self.count = lax.axis_size("row")
        self.row = lax.axis_index("row")
        self.right = self.left = own
        self.arrived = {}
        self.step = 0

    def kinds(self, k):
        return [(abs(z - (z ^ k)), int((z ^ k) > z)) for z in range(self.count)]

    def more(self):
        return self.step < self.count - 1

    def send(self):
        self.step += 1
        step, count = self.step, self.count
        to_right = [(z, z + 1) for z in range(step - 1, count - 1)]
        to_left = [(z, z - 1) for z in range(1, count - step + 1)]
        if len(dict(to_right + to_left)) == len(to_right + to_left):
            senders = [z for z, _ in to_right]
            chosen = choose([self.left, self.right], sum(self.row == z for z in senders))
            both = lax.ppermute(chosen, "row", to_right + to_left)
            return [both]
        return [
            lax.ppermute(self.right, "row", to_right),
            lax.ppermute(self.left, "row", to_left),
        ]

    def receive(self, results):
        self.right, self.left = results[0], results[-1]
        self.arrived[self.step] = (self.right, self.left)

    def ready(self, k):
        return max(step for step, _ in self.kinds(k)) <= self.step

    def slot(self, k):
        each = self.kinds(k)
        options = sorted(set(each))
        which = table_at([options.index(kind) for kind in each], self.row)
        return choose([self.arrived[step][side] for step, side in options], which)


def place_images(pieces, kind=bf16):
    me = lax.axis_index("img")
    first = pieces[0]
    width = first.shape[1]
    shape = (first.shape[0], len(pieces) * width) + first.shape[2:]
    joined = jnp.zeros(shape, kind)
    for step, piece in enumerate(pieces):
        joined = lax.dynamic_update_slice_in_dim(
            joined, piece.astype(kind), (me ^ step) * width, 1
        )
    return joined


class Chain:
    def __init__(self, value, axes):
        self.value = value
        self.todo = []
        for axis in axes:
            step = 1
            while step < lax.axis_size(axis):
                self.todo.append((axis, step))
                step *= 2

    def send(self):
        return [swap(self.value, *self.todo[0])] if self.todo else []

    def receive(self, got):
        if got:
            self.value = self.value + got[0]
            self.todo = self.todo[1:]


def sum_images(x, chain, hooks):
    count = lax.axis_size("img")
    me = lax.axis_index("img")

    def fly(index, *flights):
        sent = chain.send()
        more = hooks.get(index, lambda: [])()
        got = tie(*flights, *sent, *more)
        chain.receive(got[len(flights) : len(flights) + len(sent)])
        return got[: len(flights)], got[len(flights) + len(sent) :]

    if count != 4:
        total, kept = fly(0, lax.psum(x, "img"))
        while chain.todo:
            fly(9)
        return total[0].astype(f32), kept
    quarter = x.shape[1] // 4
    half = quarter // 2

    def piece(j, side):
        at = (me ^ j) * quarter + side * half
        return lax.dynamic_slice_in_dim(x, at, half, 1)

    def add(a, b):
        return (a.astype(f32) + b.astype(f32)).astype(bf16)

    (a_in, b_in), kept = fly(
        0,
        swap(jnp.concatenate([piece(1, 0), piece(3, 0)], axis=1), "img", 1),
        swap(jnp.concatenate([piece(2, 1), piece(3, 1)], axis=1), "img", 2),
    )
    a_own, a_far = add(piece(0, 0), a_in[:, :half]), add(piece(2, 0), a_in[:, half:])
    b_own, b_far = add(piece(0, 1), b_in[:, :half]), add(piece(1, 1), b_in[:, half:])
    (a_two, b_one), _ = fly(1, swap(a_far, "img", 2), swap(b_far, "img", 1))
    a_own, b_own = add(a_own, a_two), add(b_own, b_one)
    (a_next, b_next), _ = fly(2, swap(a_own, "img", 1), swap(b_own, "img", 2))
    (a_rest, b_rest), _ = fly(
        3,
        swap(jnp.concatenate([a_own, a_next], axis=1), "img", 2),
        swap(jnp.concatenate([b_own, b_next], axis=1), "img", 1),
    )
    while chain.todo:
        fly(9)
    parts = [
        (a_own, b_own),
        (a_next, b_rest[:, :half]),
        (a_rest[:, :half], b_next),
        (a_rest[:, half:], b_rest[:, half:]),
    ]
    return place_images([jnp.concatenate(part, axis=1) for part in parts], f32), kept


def join_cols(mine, others, axis):
    col = lax.axis_index("col")
    pieces = [mine] + list(others)
    return jnp.concatenate([choose(pieces, col ^ c) for c in range(len(pieces))], axis=axis)


def row_halo(strip):
    count = lax.axis_size("row")
    above = lax.ppermute(strip[:, -1:], "row", [(i, i + 1) for i in range(count - 1)])
    below = lax.ppermute(strip[:, :1], "row", [(i + 1, i) for i in range(count - 1)])
    return jnp.concatenate([above, strip, below], axis=1)


def on_device(
    features,
    region_boxes,
    labels,
    branch_projection_weight,
    branch_gain,
    branch_bias,
    conv_w,
    conv_gain,
    conv_bias,
    class_w,
    class_bias,
):
    _, tile_h, tile_w, channels_in = features.shape
    pixels = tile_h * tile_w
    images, row_count, col_count = (lax.axis_size(axis) for axis in ("img", "row", "col"))
    img, row, col = (lax.axis_index(axis) for axis in ("img", "row", "col"))
    groups = row_count * col_count
    block, taps, mid = conv_w.shape
    branch_width = branch_projection_weight.shape[2]
    feature_rows = channels_in // (block * col_count)
    regions = region_boxes.shape[1]
    height, width = row_count * tile_h, col_count * tile_w
    all_cells = images * height * width
    canvas_box = region_boxes[0]
    table = bin_constants(regions)
    bins = table.shape[0]
    limits = [0]
    for scale in bin_scales:
        limits.append(limits[-1] + regions * scale * scale)
    scale_rows = [
        jnp.asarray((table[:, 0] == position).astype(np.float32)) for position in range(4)
    ]

    weight = jnp.transpose(conv_w, (1, 0, 2))
    share = block // images
    rows = Rows(lax.dynamic_slice_in_dim(weight, img * share, share, 1))

    def by_line(nine):
        return [nine[3 * a : 3 * a + 3] for a in range(3)]

    weights = [by_line(weight)]
    waiting = {"cross": None, "close": None, "next": 1}

    def weight_phase(more=(), hold=()):
        flights, plan = [], []
        if rows.more():
            sent = rows.send()
            plan.append(("rows", len(sent)))
            flights += sent
        if waiting["close"] is not None:
            _, one, two = waiting["close"]
            half = share // 2
            plan.append(("close", 2))
            flights += [swap(one[:, :half], "img", 2), swap(two[:, half:], "img", 1)]
        if waiting["cross"] is not None:
            part = waiting["cross"]
            if images == 4:
                plan.append(("cross", 2))
                flights += [swap(part, "img", 1), swap(part, "img", 2)]
            else:
                plan.append(("all", images - 1))
                flights += [swap(part, "img", step) for step in range(1, images)]
        got = tie(*flights, *more, *hold)
        at = 0
        closed, crossed = waiting["close"], waiting["cross"]
        waiting["close"] = waiting["cross"] = None
        for what, count in plan:
            part = got[at : at + count]
            at += count
            if what == "rows":
                rows.receive(part)
            elif what == "close":
                pieces = closed + [jnp.concatenate(part, axis=1)]
                weights.append(
                    [place_images([piece[3 * a : 3 * a + 3] for piece in pieces]) for a in range(3)]
                )
            elif what == "cross":
                waiting["close"] = [crossed] + list(part)
            else:
                pieces = [crossed] + list(part)
                weights.append(
                    [place_images([piece[3 * a : 3 * a + 3] for piece in pieces]) for a in range(3)]
                )
        if waiting["next"] < row_count and rows.ready(waiting["next"]):
            waiting["cross"] = rows.slot(waiting["next"])
            waiting["next"] += 1
        return got[at : at + len(more)], got[at + len(more) :]

    weight_phase()

    tile = features[0].reshape(pixels, channels_in)

    def channels_of(c):
        at = [(r * col_count + c) * block for r in range(feature_rows)]
        return jnp.stack([tile[:, k : k + block] for k in at])

    by_col = [channels_of(c) for c in range(col_count)]
    sent = [
        choose(by_col, col ^ step).reshape(feature_rows, tile_h, tile_w, block)
        for step in range(col_count)
    ]
    strip = join_cols(
        sent[0], [swap(sent[step], "col", step) for step in range(1, col_count)], 2
    )
    strip_ext = row_halo(strip)

    boxes = of_bin_boxes(canvas_box, table)
    scale, bin_i, bin_j = (jnp.asarray(table[:, k]) for k in (1, 3, 4))
    extent_y, extent_x = boxes[:, 2] - boxes[:, 0], boxes[:, 3] - boxes[:, 1]
    edges = (
        boxes[:, 0] + lax.div(bin_i * extent_y, scale),
        boxes[:, 0] + lax.div((bin_i + 1) * extent_y + scale - 1, scale),
        boxes[:, 1] + lax.div(bin_j * extent_x, scale),
        boxes[:, 1] + lax.div((bin_j + 1) * extent_x + scale - 1, scale),
    )
    sizes = ((edges[1] - edges[0]) * (edges[3] - edges[2])).astype(f32)
    top, left = row * tile_h, col * tile_w
    tile_y, tile_x = grid_cells(
        top + jnp.arange(tile_h, dtype=jnp.int32), left + jnp.arange(tile_w, dtype=jnp.int32)
    )
    pooling = members(edges, tile_y, tile_x)
    local_means = dot(pooling, tile) / sizes[:, None]
    local_low = local_means.astype(bf16)
    pre_local = jnp.concatenate(
        [
            dot(
                branch_projection_weight[position],
                local_low[limits[position] : limits[position + 1]],
                (((0,), (1,)), ((), ())),
            )
            for position in range(4)
        ],
        axis=1,
    )
    pre = lax.psum_scatter(pre_local, ("row", "col"), scatter_dimension=0, tiled=True)
    part = branch_width // groups
    group = row * col_count + col

    def by_scale(value):
        return jnp.stack([jnp.sum(value * line[None], axis=1) for line in scale_rows])

    def to_bins(value):
        return sum(value[k][:, None] * scale_rows[k][None] for k in range(4))

    def branch_part(value):
        return to_bins(lax.dynamic_slice_in_dim(value, group * part, part, 1))

    counts = np.asarray([images * regions * s * s for s in bin_scales], np.float32)[:, None]
    moments = butterfly(jnp.concatenate([by_scale(pre), by_scale(pre * pre)], axis=0), ("img",))
    center = moments[:4] / counts
    inverse = lax.rsqrt(moments[4:] / counts - center * center + norm_eps)
    gain_part = branch_part(branch_gain)
    inverse_bins = to_bins(inverse)
    normed = (pre - to_bins(center)) * inverse_bins
    before = gain_part * normed + branch_part(branch_bias)
    _, (act_part,) = weight_phase(hold=[jax.nn.silu(before).astype(bf16)])
    act_branch = lax.all_gather(
        act_part, ("row", "col"), axis=0, tiled=True
    )

    def block_rows_of(r):
        first = (r * col_count + col) * block - channels_in
        position = lax.div(first, branch_width)
        taken = lax.dynamic_slice_in_dim(
            act_branch, jnp.maximum(lax.rem(first, branch_width), 0), block, 0
        )
        keep = jnp.asarray(table[:, 0]) == position
        return jnp.where(keep[None], taken, jnp.zeros((), bf16)), keep

    strip_cols = jnp.arange(width, dtype=jnp.int32)
    strip_cells = tile_h * width
    ext_cells = strip_cells + 2 * width

    def ext_spread(source):
        lines = source * tile_h - 1 + jnp.arange(tile_h + 2, dtype=jnp.int32)
        return spreads(boxes, table, *grid_cells(lines, strip_cols))

    def up_blocks(spread, r):
        return dot(spread, block_rows_of(r)[0], (((0,), (1,)), ((), ()))).astype(bf16)

    spread_ext = ext_spread(row)
    ups = jnp.stack([up_blocks(spread_ext, r) for r in range(feature_rows, row_count)])
    cat_blocks = strip_ext.reshape(feature_rows, ext_cells, block)
    slots_of = row ^ jnp.arange(row_count, dtype=jnp.int32)
    cat_wide = shifted(
        cat_blocks, canvas_box, top - 1, width, places=slots_of[:feature_rows],
        out_blocks=row_count,
    )
    cat_wide = shifted(
        ups, canvas_box, top - 1, width, places=slots_of[feature_rows:],
        out_blocks=row_count, into=cat_wide,
    )
    upper, lower = row_masks(canvas_box, jnp.arange(height, dtype=jnp.int32), strip_cols)

    def strip_of(cells, source):
        return lax.dynamic_slice_in_dim(cells, source * strip_cells, strip_cells, 0)

    keeps = [strip_of(upper, row)[:, None], None, strip_of(lower, row)[:, None]]

    (cat_moves,) = weight_phase(hold=[cat_blocks])[1]

    def moved(step, begin, end):
        to = jnp.minimum(row ^ step, feature_rows - 1)
        taken = lax.dynamic_index_in_dim(cat_moves, to, 0, keepdims=False)[begin:end]
        pairs = [(i, i ^ step) for i in range(row_count) if (i ^ step) < feature_rows]
        return lax.ppermute(taken, "row", pairs) if step else taken

    half = ext_cells // 2
    moves = []
    for step in [2, 1] + list(range(3, row_count)):
        moves += [(step, 0, half), (step, half, ext_cells)]
    landed = {(0, 0): moved(0, 0, half), (0, half): moved(0, half, ext_cells)}

    def take_moves(count):
        taken = moves[:count]
        del moves[:count]
        return taken

    def land(taken, got):
        for (step, begin, _), array in zip(taken, got):
            landed[(step, begin)] = array

    hidden_strip = 0.0
    for slot in range(row_count):
        while len(weights) <= slot:
            taken = take_moves(1 if len(moves) == 2 * (row_count - 1) else 2)
            got, hold = weight_phase(
                more=[moved(*move) for move in taken], hold=[hidden_strip] if slot else []
            )
            land(taken, got)
            if hold:
                hidden_strip = hold[0]
        for a in (1, 0, 2):
            term = dot(
                cat_wide[slot, a * width : a * width + strip_cells],
                weights[slot][a].reshape(3 * block, mid),
            )
            hidden_strip = hidden_strip + (
                term if a == 1 else jnp.where(keeps[a], term, 0.0)
            )
    own_means = lax.psum_scatter(
        local_means.astype(bf16), ("row", "col"), scatter_dimension=1, tiled=True
    )
    hidden_strip, own_means = tie(hidden_strip, own_means)
    hidden_strip = hidden_strip.reshape(tile_h, width, mid)

    def cells_of(step):
        return lax.dynamic_slice_in_dim(hidden_strip, (col ^ step) * tile_w, tile_w, 1)

    hidden = cells_of(0)
    for step in range(1, col_count):
        hidden = hidden + swap(cells_of(step), "col", step)
    hidden = hidden.reshape(pixels, mid)

    everywhere = ("col", "img", "row")
    mid_moments = butterfly(
        jnp.stack([jnp.sum(hidden, axis=0), jnp.sum(hidden * hidden, axis=0)]), everywhere
    )
    center_mid = mid_moments[0] / all_cells
    inverse_mid = lax.rsqrt(mid_moments[1] / all_cells - center_mid * center_mid + norm_eps)
    normed_mid = (hidden - center_mid) * inverse_mid
    before_mid = conv_gain * normed_mid + conv_bias
    act_mid = jax.nn.silu(before_mid).astype(bf16)
    logits = dot(act_mid, class_w) + class_bias
    classes = class_w.shape[1]
    onehot = (
        labels[0].reshape(pixels)[:, None] == jnp.arange(classes, dtype=jnp.int32)[None, :]
    ).astype(f32)
    grad_logits = (jax.nn.softmax(logits, axis=-1) - onehot).astype(bf16)
    grad_before = dot(grad_logits, class_w, contract_last) * silu_slope(before_mid)
    mid_grads = butterfly(
        jnp.stack([jnp.sum(grad_before * normed_mid, axis=0), jnp.sum(grad_before, axis=0)]),
        everywhere,
    )
    conv_gain_grad, conv_bias_grad = mid_grads[0], mid_grads[1]
    class_chain = Chain(
        jnp.concatenate(
            [
                dot(act_mid, grad_logits, contract_first),
                jnp.sum(grad_logits.astype(f32), axis=0, keepdims=True),
            ],
            axis=0,
        ),
        everywhere,
    )
    grad_hidden = (
        conv_gain
        * inverse_mid
        * (grad_before - conv_bias_grad / all_cells - normed_mid * conv_gain_grad / all_cells)
    ).astype(bf16)

    grad_tile = grad_hidden.reshape(tile_h, tile_w, mid)
    grad_strip = join_cols(
        grad_tile, [swap(grad_tile, "col", step) for step in range(1, col_count)], 1
    )
    hops = Rows(grad_tile)
    grad_ext = row_halo(grad_strip[None]).reshape(1, ext_cells, mid)
    own_wide = shifted(grad_ext, canvas_box, top - 1, width, reverse=True)[0]

    def input_grads(slot):
        sums = []
        for a in range(3):
            sums.append(
                sum(
                    dot(
                        own_wide[a * width : a * width + strip_cells, j * mid : (j + 1) * mid],
                        weights[slot][2 - a][j],
                        contract_last,
                    )
                    for j in range(3)
                )
            )
        total = sums[1] + jnp.where(keeps[0], sums[0], 0.0) + jnp.where(keeps[2], sums[2], 0.0)
        return total.astype(bf16)

    conv_sums = [0.0] * taps

    def weight_grads(slot, strip):
        source = row ^ slot
        ext = jnp.where(
            row < feature_rows,
            jnp.concatenate([landed[(slot, 0)], landed[(slot, half)]], axis=0),
            up_blocks(ext_spread(source), row),
        )
        if slot == 0:
            wide = own_wide[width : width + strip_cells]
        else:
            wide = shifted(
                strip.reshape(1, strip_cells, mid), canvas_box, source * tile_h, width,
                reverse=True,
            )[0]
        masks = [strip_of(upper, source), None, strip_of(lower, source)]
        for a in range(3):
            side = ext[a * width : a * width + strip_cells]
            if a != 1:
                side = jnp.where(masks[a][:, None], side, jnp.zeros((), bf16))
            for j in range(3):
                conv_sums[3 * a + j] = conv_sums[3 * a + j] + dot(
                    side, wide[:, j * mid : (j + 1) * mid], contract_first
                )

    cat_grads, strips, swapping, asked = [], {0: grad_strip}, None, 1
    while len(strips) < row_count:
        flights, plan = [], []
        if hops.more():
            sent = hops.send()
            plan.append(("hops", len(sent)))
            flights += sent
        if swapping is not None:
            plan.append(("swap", col_count - 1))
            flights += [swap(swapping[1], "col", step) for step in range(1, col_count)]
        taken = take_moves(1)
        plan.append(("moves", len(taken)))
        flights += [moved(*move) for move in taken]
        sent = class_chain.send()
        plan.append(("class", len(sent)))
        flights += sent
        held = [input_grads(len(cat_grads))] if len(cat_grads) < row_count else []
        if len(cat_grads) + 1 < row_count and len(cat_grads) > 0:
            held.append(input_grads(len(cat_grads) + 1))
        got = tie(*flights, *held)
        cat_grads += got[len(flights) :]
        at = 0
        swapped, swapping = swapping, None
        for what, count in plan:
            part = got[at : at + count]
            at += count
            if what == "hops":
                hops.receive(part)
            elif what == "swap":
                strips[swapped[0]] = join_cols(swapped[1], part, 1)
            elif what == "moves":
                land(taken, part)
            else:
                class_chain.receive(part)
        if asked < row_count and hops.ready(asked):
            swapping = (asked, hops.slot(asked))
            asked += 1
    while moves:
        taken = take_moves(2)
        land(taken, [moved(*move) for move in taken])
    while len(cat_grads) < row_count:
        cat_grads.append(input_grads(len(cat_grads)))
    by_row = [choose(cat_grads, row ^ r) for r in range(row_count)]
    for slot in range(row_count):
        weight_grads(slot, strips[slot])
    conv_term = jnp.stack(conv_sums).astype(bf16)
    spread_strip = lax.slice_in_dim(spread_ext, width, width + strip_cells, axis=1)
    grad_bins_local = jnp.zeros((branch_width, bins), f32)
    for r in range(feature_rows, row_count):
        first = (r * col_count + col) * block - channels_in
        keep = jnp.asarray(table[:, 0]) == lax.div(first, branch_width)
        terms = dot(by_row[r], spread_strip, (((0,), (1,)), ((), ())))
        terms = jnp.where(keep[None], terms, 0.0)
        at = lax.rem(first, branch_width)
        old = lax.dynamic_slice_in_dim(grad_bins_local, at, block, 0)
        grad_bins_local = lax.dynamic_update_slice_in_dim(grad_bins_local, old + terms, at, 0)
    grad_bins = lax.psum_scatter(
        grad_bins_local, ("row", "col"), scatter_dimension=0, tiled=True
    )
    grad_act = grad_bins * silu_slope(before)
    branch_sums = butterfly(
        jnp.concatenate([by_scale(grad_act * normed), by_scale(grad_act)], axis=0), ("img",)
    )
    grad_pre = (
        gain_part
        * inverse_bins
        * (
            grad_act
            - to_bins(branch_sums[4:] / counts)
            - normed * to_bins(branch_sums[:4] / counts)
        )
    ).astype(bf16)
    conv_w_grad, (grad_pre, branch_sums) = sum_images(
        conv_term, class_chain, {0: lambda: [grad_pre, branch_sums]}
    )
    class_w_grad, class_bias_grad = class_chain.value[:mid], class_chain.value[mid]
    gathered = lax.all_gather(
        jnp.concatenate([grad_pre.astype(f32), branch_sums.T], axis=1),
        ("row", "col"), axis=0, tiled=True,
    )
    grad_pre = gathered[:, :bins].astype(bf16)
    branch_all = gathered[:, bins:].T
    branch_gain_grad, branch_bias_grad = branch_all[:4], branch_all[4:]

    weight_terms, bin_grads = [], []
    for position in range(4):
        span = slice(limits[position], limits[position + 1])
        weight_terms.append(
            dot(own_means[span], grad_pre[:, span], (((0,), (1,)), ((), ())))
        )
        bin_grads.append(
            dot(grad_pre[:, span], branch_projection_weight[position], (((0,), (1,)), ((), ())))
        )
    bin_grads = (jnp.concatenate(bin_grads, axis=0) / sizes[:, None]).astype(bf16)
    grad_pool = dot(pooling, bin_grads, contract_first)

    own_features = [
        by_row[r].reshape(tile_h, width, block) for r in range(feature_rows)
    ]

    def feature_grads_of(step):
        return jnp.stack(
            [
                choose(
                    [one[:, c * tile_w : (c + 1) * tile_w] for c in range(col_count)], col ^ step
                ).reshape(pixels, block)
                for one in own_features
            ]
        )

    by_step = [feature_grads_of(0)] + [
        swap(feature_grads_of(step), "col", step) for step in range(1, col_count)
    ]
    by_block = [choose(by_step, col ^ c) for c in range(col_count)]
    joined = jnp.concatenate(
        [by_block[c][r] for r in range(feature_rows) for c in range(col_count)], axis=1
    )
    feature_grad = (joined.astype(f32) + grad_pool).reshape(1, tile_h, tile_w, channels_in)

    branch_w_grad = lax.psum(jnp.stack(weight_terms).astype(bf16), "img").astype(f32)
    conv_w_grad = jnp.transpose(conv_w_grad, (1, 0, 2))
    return (
        logits.reshape(1, tile_h, tile_w, classes),
        feature_grad,
        branch_w_grad,
        branch_gain_grad,
        branch_bias_grad,
        conv_w_grad,
        conv_gain_grad,
        conv_bias_grad,
        class_w_grad,
        class_bias_grad,
    )


def solution(mesh):
    return jax.shard_map(
        on_device,
        mesh=mesh,
        in_specs=(
            P("img", "row", "col", None),
            P("img", None, None),
            P("img", "row", "col"),
            P(),
            P(),
            P(),
            P(("row", "col"), None, None),
            P(),
            P(),
            P(),
            P(),
        ),
        out_specs=(
            P("img", "row", "col", None),
            P("img", "row", "col", None),
            P(None, ("row", "col"), None),
            P(),
            P(),
            P(("row", "col"), None, None),
            P(),
            P(),
            P(),
            P(),
        ),
        check_vma=False,
    )
```

```python
import jax
import jax.numpy as jnp
import numpy as np
from jax import lax
from jax.experimental import pallas as pl
from jax.experimental.pallas import tpu as pltpu
from jax.sharding import PartitionSpec as P

bin_scales = (1, 2, 3, 6)
norm_eps = 1e-05
tap_offsets = ((-1, -1), (-1, 0), (-1, 1), (0, -1), (0, 0), (0, 1), (1, -1), (1, 0), (1, 1))
contract_first = (((0,), (0,)), ((), ()))
contract_last = (((1,), (1,)), ((), ()))
bf16 = jnp.bfloat16
f32 = jnp.float32


def dot(a, b, dims=(((1,), (0,)), ((), ()))):
    return lax.dot_general(a, b, dims, preferred_element_type=f32)


def swap(value, axis, step):
    count = lax.axis_size(axis)
    return lax.ppermute(value, axis, [(i, i ^ step) for i in range(count)])


def butterfly(value, axes):
    for axis in axes:
        step = 1
        while step < lax.axis_size(axis):
            value = value + swap(value, axis, step)
            step *= 2
    return value


def bin_constants(regions):
    rows = []
    for position, scale in enumerate(bin_scales):
        for r in range(regions):
            for i in range(scale):
                for j in range(scale):
                    rows.append((position, scale, r, i, j))
    return np.asarray(rows, np.int32)


def of_bin_boxes(canvas_box, table):
    pick = jnp.asarray(table[:, 2:3] == np.arange(canvas_box.shape[0])[None, :], jnp.int32)
    return jnp.sum(pick[:, :, None] * canvas_box[None], axis=1)


def members(edges, cells_y, cells_x):
    lo_y, hi_y, lo_x, hi_x = (edge[:, None] for edge in edges)
    y, x = cells_y[None, :], cells_x[None, :]
    return ((y >= lo_y) & (y < hi_y) & (x >= lo_x) & (x < hi_x)).astype(bf16)


def axis_weight(cells, first, last, scale, index):
    extent = (last - first - 1).astype(f32)[:, None]
    place = ((cells[None, :] - first[:, None]) * (scale - 1)[:, None]).astype(f32)
    away = jnp.abs(place - index.astype(f32)[:, None] * extent) / extent
    inside = (cells[None, :] >= first[:, None]) & (cells[None, :] < last[:, None])
    return jnp.where(inside, jnp.maximum(1.0 - away, 0.0), 0.0)


def spreads(boxes, table, cells_y, cells_x):
    scale, i, j = (jnp.asarray(table[:, k]) for k in (1, 3, 4))
    weight_y = axis_weight(cells_y, boxes[:, 0], boxes[:, 2], scale, i)
    weight_x = axis_weight(cells_x, boxes[:, 1], boxes[:, 3], scale, j)
    return (weight_y * weight_x).astype(bf16)


def grid_cells(rows, cols):
    y = jnp.broadcast_to(rows[:, None], (rows.shape[0], cols.shape[0])).reshape(-1)
    x = jnp.broadcast_to(cols[None, :], (rows.shape[0], cols.shape[0])).reshape(-1)
    return y, x


def row_masks(canvas_box, rows, cols):
    y, x = rows[:, None], cols[None, :]
    up, left, down, right = (canvas_box[:, k][:, None, None] for k in range(4))
    inside = (y >= up) & (y < down) & (x >= left) & (x < right)
    upper = jnp.any(inside & (y > up), axis=0)
    lower = jnp.any(inside & (y + 1 < down), axis=0)
    return upper.reshape(-1), lower.reshape(-1)


small_cost = pl.CostEstimate(flops=1024, bytes_accessed=1024, transcendentals=0)


def shift_lines(box_ref, first, x_ref, o_ref, width, reverse):
    cells, block = x_ref.shape
    order = (2, 1, 0) if reverse else (0, 1, 2)
    left_at, mid_at, right_at = (place * block for place in order)

    def line(at, carry):
        y = first + at
        here = pl.ds(pl.multiple_of(at * width, width), width)
        x = lax.broadcasted_iota(jnp.int32, (width, block), 0)
        no_left = x == 0
        no_right = x == width - 1
        for r in range(box_ref.shape[0]):
            inside = (y >= box_ref[r, 0]) & (y < box_ref[r, 2])
            no_left = no_left | (x == jnp.where(inside, box_ref[r, 1], -1))
            no_right = no_right | (x == jnp.where(inside, box_ref[r, 3] - 1, -1))
        own = x_ref[here, :]
        wide = own.astype(f32)
        left = jnp.where(no_left, 0.0, pltpu.roll(wide, 1, 0))
        right = jnp.where(no_right, 0.0, pltpu.roll(wide, width - 1, 0))
        o_ref[here, left_at : left_at + block] = left.astype(bf16)
        o_ref[here, mid_at : mid_at + block] = own
        o_ref[here, right_at : right_at + block] = right.astype(bf16)
        return carry

    lax.fori_loop(0, cells // width, line, 0)


def shifted(x, canvas_box, first_line, width, reverse=False, places=None, out_blocks=1, into=None):
    blocks, cells, block = x.shape
    total = cells // width
    lines = max(k for k in range(1, total + 1) if total % k == 0 and k * width <= 2048)
    if places is None:
        places, out_blocks = jnp.arange(blocks, dtype=jnp.int32), blocks

    def body(place_ref, first_ref, box_ref, x_ref, *rest):
        first = first_ref[0] + pl.program_id(1) * lines
        shift_lines(box_ref, first, x_ref.at[0], rest[-1].at[0], width, reverse)

    extra = [] if into is None else [into]
    return pl.pallas_call(
        body,
        grid_spec=pltpu.PrefetchScalarGridSpec(
            num_scalar_prefetch=2,
            grid=(blocks, total // lines),
            in_specs=[
                pl.BlockSpec(memory_space=pltpu.SMEM),
                pl.BlockSpec((1, width * lines, block), lambda b, i, at, first: (b, i, 0)),
            ]
            + [pl.BlockSpec(memory_space=pl.ANY)] * len(extra),
            out_specs=pl.BlockSpec(
                (1, width * lines, 3 * block), lambda b, i, at, first: (at[b], i, 0)
            ),
        ),
        out_shape=jax.ShapeDtypeStruct((out_blocks, cells, 3 * block), bf16),
        input_output_aliases={4: 0} if extra else {},
        compiler_params=pltpu.CompilerParams(vmem_limit_bytes=52 << 20),
        cost_estimate=small_cost,
    )(places, jnp.reshape(first_line, (1,)).astype(jnp.int32), canvas_box, x, *extra)


def chunk_of(cells, width):
    total = cells // width
    return max(k for k in range(1, total + 1) if total % k == 0 and k * width <= 1024) * width


def conv_slot(wide, slot, weight, keeps, total, width):
    _, ext, deep = wide.shape
    _, block, mid = weight[0].shape
    cells = keeps.shape[1]
    chunk = chunk_of(cells, width)

    def body(x_ref, *rest):
        w_refs, keep_ref, o_ref = rest[:3], rest[3], rest[-1]
        begin = pl.program_id(0) * chunk
        value = 0.0 if total is None else rest[4][...]
        for a in range(3):
            term = jnp.dot(
                x_ref[0, pl.ds(pl.multiple_of(begin + a * width, width), chunk), :],
                w_refs[a][...].reshape(3 * block, mid),
                preferred_element_type=f32,
            )
            value = value + (term if a == 1 else keep_ref[a] * term)
        o_ref[...] = value

    extra = [] if total is None else [total]
    once = pl.Buffered(1)
    one = pl.BlockSpec((3, block, mid), lambda c: (0, 0, 0), pipeline_mode=once)
    return pl.pallas_call(
        body,
        grid=(cells // chunk,),
        in_specs=[
            pl.BlockSpec((1, ext, deep), lambda c: (slot, 0, 0), pipeline_mode=once),
            one, one, one,
            pl.BlockSpec((3, chunk, 1), lambda c: (0, c, 0)),
        ]
        + [pl.BlockSpec((chunk, mid), lambda c: (c, 0))] * len(extra),
        out_specs=pl.BlockSpec((chunk, mid), lambda c: (c, 0)),
        out_shape=jax.ShapeDtypeStruct((cells, mid), f32),
        input_output_aliases={5: 0} if extra else {},
        compiler_params=pltpu.CompilerParams(vmem_limit_bytes=32 << 20),
        cost_estimate=small_cost,
    )(wide, *weight, keeps, *extra)


def grad_slot(wide, weight, keeps, width, marker=None):
    ext, deep = wide.shape
    _, block, mid = weight[0].shape
    cells = keeps.shape[1]
    chunk = chunk_of(cells, width)

    def body(x_ref, *rest):
        w_refs, keep_ref, o_ref = rest[:3], rest[3], rest[-1]
        begin = pl.program_id(0) * chunk
        value = 0.0
        for a in range(3):
            rows = pl.ds(pl.multiple_of(begin + a * width, width), chunk)
            term = 0.0
            for j in range(3):
                term = term + lax.dot_general(
                    x_ref[rows, j * mid : (j + 1) * mid],
                    w_refs[2 - a][j],
                    contract_last,
                    preferred_element_type=f32,
                )
            value = value + (term if a == 1 else keep_ref[a] * term)
        o_ref[...] = value.astype(bf16)

    extra = [] if marker is None else [marker]
    once = pl.Buffered(1)
    one = pl.BlockSpec((3, block, mid), lambda c: (0, 0, 0), pipeline_mode=once)
    return pl.pallas_call(
        body,
        grid=(cells // chunk,),
        in_specs=[
            pl.BlockSpec((ext, deep), lambda c: (0, 0), pipeline_mode=once),
            one, one, one,
            pl.BlockSpec((3, chunk, 1), lambda c: (0, c, 0)),
        ]
        + [pl.BlockSpec(memory_space=pl.ANY)] * len(extra),
        out_specs=pl.BlockSpec((chunk, block), lambda c: (c, 0)),
        out_shape=jax.ShapeDtypeStruct((cells, block), bf16),
        compiler_params=pltpu.CompilerParams(vmem_limit_bytes=32 << 20),
        cost_estimate=small_cost,
    )(wide, *weight, keeps, *extra)


def silu_slope(value):
    sigmoid_value = jax.nn.sigmoid(value)
    return sigmoid_value * (1.0 + value * (1.0 - sigmoid_value))


def choose(options, index):
    value = options[0]
    for k in range(1, len(options)):
        value = jnp.where(index == k, options[k], value)
    return value


def table_at(values, index):
    return choose([jnp.int32(value) for value in values], index)


def tie(*arrays):
    return list(lax.optimization_barrier(tuple(arrays)))


class Rows:
    def __init__(self, own):
        self.count = lax.axis_size("row")
        self.row = lax.axis_index("row")
        self.right = self.left = own
        self.arrived = {}
        self.step = 0

    def kinds(self, k):
        return [(abs(z - (z ^ k)), int((z ^ k) > z)) for z in range(self.count)]

    def more(self):
        return self.step < self.count - 1

    def send(self):
        self.step += 1
        step, count = self.step, self.count
        to_right = [(z, z + 1) for z in range(step - 1, count - 1)]
        to_left = [(z, z - 1) for z in range(1, count - step + 1)]
        return [
            lax.ppermute(self.right, "row", to_right),
            lax.ppermute(self.left, "row", to_left),
        ]

    def receive(self, results):
        self.right, self.left = results[0], results[-1]
        self.arrived[self.step] = (self.right, self.left)

    def ready(self, k):
        return max(step for step, _ in self.kinds(k)) <= self.step

    def slot(self, k):
        each = self.kinds(k)
        options = sorted(set(each))
        which = table_at([options.index(kind) for kind in each], self.row)
        return choose([self.arrived[step][side] for step, side in options], which)


def place_images(pieces, kind=bf16):
    me = lax.axis_index("img")
    first = pieces[0]
    width = first.shape[1]
    shape = (first.shape[0], len(pieces) * width) + first.shape[2:]
    joined = jnp.zeros(shape, kind)
    for step, piece in enumerate(pieces):
        joined = lax.dynamic_update_slice_in_dim(
            joined, piece.astype(kind), (me ^ step) * width, 1
        )
    return joined


class Chain:
    def __init__(self, value, axes):
        self.value = value
        self.todo = []
        for axis in axes:
            step = 1
            while step < lax.axis_size(axis):
                self.todo.append((axis, step))
                step *= 2

    def send(self):
        return [swap(self.value, *self.todo[0])] if self.todo else []

    def receive(self, got):
        if got:
            self.value = self.value + got[0]
            self.todo = self.todo[1:]


def mark(*arrays):
    tiny = jnp.zeros((8, 128), f32)
    *arrays, tiny = tie(*arrays, tiny)
    return arrays, swap(tiny, "col", 1)


def add_low(a, b):
    return (a.astype(f32) + b.astype(f32)).astype(bf16)


class ImageSum:
    def __init__(self, x):
        self.x = x
        self.me = lax.axis_index("img")
        self.half = x.shape[1] // 8

    def piece(self, j, side):
        at = (self.me ^ j) * 2 * self.half + side * self.half
        return lax.dynamic_slice_in_dim(self.x, at, self.half, 1)

    def first_sends(self):
        return [
            jnp.concatenate([self.piece(1, 0), self.piece(3, 0)], axis=1),
            jnp.concatenate([self.piece(2, 1), self.piece(3, 1)], axis=1),
        ]

    def first(self, sends):
        return [swap(sends[0], "img", 1), swap(sends[1], "img", 2)]

    def second_sends(self, got):
        half = self.half
        self.own = [add_low(self.piece(0, k), got[k][:, :half]) for k in range(2)]
        return [
            add_low(self.piece(2, 0), got[0][:, half:]),
            add_low(self.piece(1, 1), got[1][:, half:]),
        ]

    def second(self, sends):
        return [swap(sends[0], "img", 2), swap(sends[1], "img", 1)]

    def reduced(self, got):
        self.own = [add_low(a, b) for a, b in zip(self.own, got)]
        return self.own

    def third(self, own):
        self.own = own
        return [swap(own[0], "img", 1), swap(own[1], "img", 2)]

    def fourth_sends(self, got):
        self.next = got
        return [jnp.concatenate([own, near], axis=1) for own, near in zip(self.own, got)]

    def fourth(self, sends):
        return [swap(sends[0], "img", 2), swap(sends[1], "img", 1)]

    def gathered(self, got):
        half = self.half
        parts = [
            (self.own[0], self.own[1]),
            (self.next[0], got[1][:, :half]),
            (got[0][:, :half], self.next[1]),
            (got[0][:, half:], got[1][:, half:]),
        ]
        return place_images([jnp.concatenate(part, axis=1) for part in parts], f32)


def join_cols(mine, others, axis):
    col = lax.axis_index("col")
    pieces = [mine] + list(others)
    return jnp.concatenate([choose(pieces, col ^ c) for c in range(len(pieces))], axis=axis)


def row_halo(lines):
    count = lax.axis_size("row")
    above = lax.ppermute(lines[-1:], "row", [(i, i + 1) for i in range(count - 1)])
    below = lax.ppermute(lines[:1], "row", [(i + 1, i) for i in range(count - 1)])
    return jnp.concatenate([above, lines, below], axis=0)


def on_device(
    features,
    region_boxes,
    labels,
    branch_projection_weight,
    branch_gain,
    branch_bias,
    conv_w,
    conv_gain,
    conv_bias,
    class_w,
    class_bias,
):
    _, tile_h, tile_w, channels_in = features.shape
    pixels = tile_h * tile_w
    images, row_count, col_count = (lax.axis_size(axis) for axis in ("img", "row", "col"))
    img, row, col = (lax.axis_index(axis) for axis in ("img", "row", "col"))
    groups = row_count * col_count
    block, taps, mid = conv_w.shape
    branch_width = branch_projection_weight.shape[2]
    feature_rows = channels_in // (block * col_count)
    regions = region_boxes.shape[1]
    height, width = row_count * tile_h, col_count * tile_w
    all_cells = images * height * width
    canvas_box = region_boxes[0]
    table = bin_constants(regions)
    bins = table.shape[0]
    limits = [0]
    for scale in bin_scales:
        limits.append(limits[-1] + regions * scale * scale)
    scale_rows = [
        jnp.asarray((table[:, 0] == position).astype(np.float32)) for position in range(4)
    ]

    weight = jnp.transpose(conv_w, (1, 0, 2))
    share = block // images
    own_share, tile = tie(
        lax.dynamic_slice_in_dim(weight, img * share, share, 1),
        features[0].reshape(pixels, channels_in),
    )
    rows = Rows(own_share)

    def by_line(nine):
        return [nine[3 * a : 3 * a + 3] for a in range(3)]

    weights = [by_line(weight)]
    waiting = {"next": 1, "send": [], "plan": [], "slot": None, "place": []}

    def weight_plan(before=()):
        plan, send = [], [[], []]
        if waiting["slot"] is not None:
            pieces = waiting["slot"]
            half = share // 2
            send[0].append(pieces[2][:, half:])
            send[1].append(pieces[1][:, :half])
            plan.append(("close", pieces))
        if waiting["next"] < row_count and rows.ready(waiting["next"]):
            part = rows.slot(waiting["next"])
            waiting["next"] += 1
            send[0].append(part)
            send[1].append(part)
            plan.append(("cross", part))
        send = [jnp.concatenate(arrays, axis=1) for arrays in send if arrays]
        placed = waiting["place"] if plan else []
        got, waiting["mark"] = mark(*send, *before, *placed)
        waiting["send"], waiting["plan"] = got[: len(send)], plan
        end = len(got) - len(placed)
        place_now(got[end:] if plan else waiting["place"])
        return got[len(send) : end]

    def lines_of(pieces):
        return [place_images([piece[3 * a : 3 * a + 3] for piece in pieces]) for a in range(3)]

    def place_now(pieces):
        if pieces:
            weights.append(lines_of(pieces))
        waiting["place"] = []

    def weight_phase(more=(), hold=()):
        flights = [swap(send, "img", k + 1) for k, send in enumerate(waiting["send"])]
        count = len(flights)
        hop = waiting["hop"]
        flights += hop
        got = tie(*flights, *more, *hold)
        if hop:
            rows.receive(got[count : len(flights)])
        waiting["hop"] = rows.send() if rows.more() else []
        waiting["slot"] = None
        at = 0
        for what, kept in waiting["plan"]:
            size = share // 2 if what == "close" else share
            part = [array[:, at : at + size] for array in got[:count]]
            at += size
            if what == "close":
                far = jnp.concatenate([part[1], part[0]], axis=1)
                waiting["place"] = kept + [far]
            else:
                waiting["slot"] = [kept] + part
        at = len(flights)
        return got[at : at + len(more)], got[at + len(more) :]

    waiting["hop"] = rows.send()

    tile_ext = row_halo(tile.reshape(tile_h, tile_w, channels_in))

    def channels_of(c):
        at = [(r * col_count + c) * block for r in range(feature_rows)]
        return jnp.stack([tile_ext[..., k : k + block] for k in at])

    by_col = [channels_of(c) for c in range(col_count)]
    sent = [choose(by_col, col ^ step) for step in range(col_count)]
    strip_ext = join_cols(
        sent[0], [swap(sent[step], "col", step) for step in range(1, col_count)], 2
    )
    weight_phase()
    (strip_ext,) = weight_plan([strip_ext])

    boxes = of_bin_boxes(canvas_box, table)
    scale, bin_i, bin_j = (jnp.asarray(table[:, k]) for k in (1, 3, 4))
    extent_y, extent_x = boxes[:, 2] - boxes[:, 0], boxes[:, 3] - boxes[:, 1]
    edges = (
        boxes[:, 0] + lax.div(bin_i * extent_y, scale),
        boxes[:, 0] + lax.div((bin_i + 1) * extent_y + scale - 1, scale),
        boxes[:, 1] + lax.div(bin_j * extent_x, scale),
        boxes[:, 1] + lax.div((bin_j + 1) * extent_x + scale - 1, scale),
    )
    sizes = ((edges[1] - edges[0]) * (edges[3] - edges[2])).astype(f32)
    top, left = row * tile_h, col * tile_w
    tile_y, tile_x = grid_cells(
        top + jnp.arange(tile_h, dtype=jnp.int32), left + jnp.arange(tile_w, dtype=jnp.int32)
    )
    pooling = members(edges, tile_y, tile_x)
    local_means = dot(pooling, tile) / sizes[:, None]
    local_low = local_means.astype(bf16)
    pre_local = jnp.concatenate(
        [
            dot(
                branch_projection_weight[position],
                local_low[limits[position] : limits[position + 1]],
                (((0,), (1,)), ((), ())),
            )
            for position in range(4)
        ],
        axis=1,
    )
    pre = lax.psum_scatter(pre_local, ("row", "col"), scatter_dimension=0, tiled=True)
    cat_blocks = strip_ext.reshape(feature_rows, -1, block)
    slots_of = row ^ jnp.arange(row_count, dtype=jnp.int32)
    cat_wide = shifted(
        cat_blocks, canvas_box, top - 1, width, places=slots_of[:feature_rows],
        out_blocks=row_count,
    )
    _, (pre, cat_wide) = weight_phase(hold=[pre, cat_wide])
    part = branch_width // groups
    group = row * col_count + col

    def by_scale(value):
        return jnp.stack([jnp.sum(value * line[None], axis=1) for line in scale_rows])

    def to_bins(value):
        return sum(value[k][:, None] * scale_rows[k][None] for k in range(4))

    def branch_part(value):
        return to_bins(lax.dynamic_slice_in_dim(value, group * part, part, 1))

    counts = np.asarray([images * regions * s * s for s in bin_scales], np.float32)[:, None]
    moments = butterfly(jnp.concatenate([by_scale(pre), by_scale(pre * pre)], axis=0), ("img",))
    moments, cat_wide = weight_plan([moments, cat_wide])
    center = moments[:4] / counts
    inverse = lax.rsqrt(moments[4:] / counts - center * center + norm_eps)
    gain_part = branch_part(branch_gain)
    inverse_bins = to_bins(inverse)
    normed = (pre - to_bins(center)) * inverse_bins
    before = gain_part * normed + branch_part(branch_bias)
    act_branch = lax.all_gather(
        (jax.nn.silu(before) + waiting["mark"][0, 0]).astype(bf16),
        ("row", "col"), axis=0, tiled=True,
    )

    def block_rows_of(r):
        first = (r * col_count + col) * block - channels_in
        position = lax.div(first, branch_width)
        taken = lax.dynamic_slice_in_dim(
            act_branch, jnp.maximum(lax.rem(first, branch_width), 0), block, 0
        )
        keep = jnp.asarray(table[:, 0]) == position
        return jnp.where(keep[None], taken, jnp.zeros((), bf16)), keep

    strip_cols = jnp.arange(width, dtype=jnp.int32)
    strip_cells = tile_h * width
    ext_cells = strip_cells + 2 * width

    def ext_spread(source):
        lines = source * tile_h - 1 + jnp.arange(tile_h + 2, dtype=jnp.int32)
        return spreads(boxes, table, *grid_cells(lines, strip_cols))

    def up_blocks(spread, r):
        return dot(spread, block_rows_of(r)[0], (((0,), (1,)), ((), ()))).astype(bf16)

    spread_ext = ext_spread(row)
    ups = jnp.stack([up_blocks(spread_ext, r) for r in range(feature_rows, row_count)])
    cat_wide = shifted(
        ups, canvas_box, top - 1, width, places=slots_of[feature_rows:],
        out_blocks=row_count, into=cat_wide,
    )
    upper, lower = row_masks(canvas_box, jnp.arange(height, dtype=jnp.int32), strip_cols)

    def strip_of(cells, source):
        return lax.dynamic_slice_in_dim(cells, source * strip_cells, strip_cells, 0)

    keeps = jnp.stack(
        [strip_of(upper, row), jnp.ones((strip_cells,), bool), strip_of(lower, row)]
    ).astype(f32)[:, :, None]

    depth = row_count // 2
    place = lax.rem(row, depth)
    _, (cat_wide, cat_blocks) = weight_phase(hold=[cat_wide, cat_blocks])

    def moved(step):
        return lax.dynamic_index_in_dim(cat_blocks, place ^ step, 0, keepdims=False)

    own_ext, *sends, cat_wide = weight_plan([moved(step) for step in range(depth)] + [cat_wide])
    feature_exts = {0: own_ext}
    hidden_strip = conv_slot(cat_wide, 0, weights[0], keeps, None, width)
    for slot in range(1, row_count):
        while len(weights) <= slot:
            step = len(feature_exts)
            more = [swap(sends[step - 1], "row", step)] if step < depth else []
            got, hold = weight_phase(more=more, hold=[hidden_strip])
            if got:
                feature_exts[step] = got[0]
            (hidden_strip,) = weight_plan(hold)
        hidden_strip = conv_slot(cat_wide, slot, weights[slot], keeps, hidden_strip, width)
    for step in range(1, depth):
        if step not in feature_exts:
            feature_exts[step] = swap(sends[step - 1], "row", step)
    hidden_strip = hidden_strip.reshape(tile_h, width, mid)

    def cells_of(step):
        return lax.dynamic_slice_in_dim(hidden_strip, (col ^ step) * tile_w, tile_w, 1)

    hidden = cells_of(0)
    for step in range(1, col_count):
        hidden = hidden + swap(cells_of(step), "col", step)
    hidden = hidden.reshape(pixels, mid)

    everywhere = ("col", "img", "row")
    mid_moments = butterfly(
        jnp.stack([jnp.sum(hidden, axis=0), jnp.sum(hidden * hidden, axis=0)]), everywhere
    )
    center_mid = mid_moments[0] / all_cells
    inverse_mid = lax.rsqrt(mid_moments[1] / all_cells - center_mid * center_mid + norm_eps)
    normed_mid = (hidden - center_mid) * inverse_mid
    before_mid = conv_gain * normed_mid + conv_bias
    act_mid = jax.nn.silu(before_mid).astype(bf16)
    logits = dot(act_mid, class_w) + class_bias
    classes = class_w.shape[1]
    onehot = (
        labels[0].reshape(pixels)[:, None] == jnp.arange(classes, dtype=jnp.int32)[None, :]
    ).astype(f32)
    grad_logits = (jax.nn.softmax(logits, axis=-1) - onehot).astype(bf16)
    grad_before = dot(grad_logits, class_w, contract_last) * silu_slope(before_mid)
    mid_grads = butterfly(
        jnp.stack([jnp.sum(grad_before * normed_mid, axis=0), jnp.sum(grad_before, axis=0)]),
        everywhere,
    )
    conv_gain_grad, conv_bias_grad = mid_grads[0], mid_grads[1]
    background = ("col", "row", "img")
    class_chain = Chain(
        jnp.concatenate(
            [
                dot(act_mid, grad_logits, contract_first),
                jnp.sum(grad_logits.astype(f32), axis=0, keepdims=True),
            ],
            axis=0,
        ),
        background,
    )
    grad_hidden = (
        conv_gain
        * inverse_mid
        * (grad_before - conv_bias_grad / all_cells - normed_mid * conv_gain_grad / all_cells)
    ).astype(bf16)

    def pair_strip(mine):
        return [swap(mine, "col", step) for step in range(1, col_count)]

    grad_hidden, mean_moves = tie(grad_hidden, local_means.astype(bf16))
    own_means = lax.psum_scatter(mean_moves, ("row", "col"), scatter_dimension=1, tiled=True)
    grad_tile = grad_hidden.reshape(tile_h, tile_w, mid)
    hops = [swap(grad_tile, "row", step) for step in range(1, depth)]
    grad_ext = row_halo(grad_tile)
    grad_ext = join_cols(grad_ext, pair_strip(grad_ext), 1)
    grad_strip = grad_ext[1:-1]
    grad_ext = grad_ext.reshape(1, ext_cells, mid)
    own_wide = shifted(grad_ext, canvas_box, top - 1, width, reverse=True)[0]

    def input_grads(slot, marker=None):
        return grad_slot(own_wide, weights[slot], keeps, width, marker)

    low_zero = jnp.zeros((), bf16)
    lower_half = row < depth
    up_exts = [choose([ups[r] for r in range(depth)], place)] + [
        up_blocks(ext_spread(row ^ step), feature_rows + place) for step in range(1, depth)
    ]
    exts = [
        (
            jnp.where(lower_half, up_exts[step], feature_exts[step]),
            jnp.where(lower_half, feature_exts[step], up_exts[step]),
        )
        for step in range(depth)
    ]
    sides = []
    for kind in range(2):
        lines = []
        for a in range(3):
            pieces = []
            for step in range(depth):
                piece = exts[step][kind][a * width : a * width + strip_cells]
                if a != 1:
                    keep = strip_of((upper, None, lower)[a], row ^ step)
                    piece = jnp.where(keep[:, None], piece, low_zero)
                pieces.append(piece)
            lines.append(jnp.concatenate(pieces, axis=0))
        sides.append(lines)

    def phase(flights, hold=()):
        sent = class_chain.send()
        got = tie(*flights, *sent, *hold)
        class_chain.receive(got[len(flights) : len(flights) + len(sent)])
        return got[: len(flights)], got[len(flights) + len(sent) :]

    wides = shifted(
        grad_strip.reshape(1, strip_cells, mid), canvas_box, top, width, reverse=True,
        places=jnp.zeros((1,), jnp.int32), out_blocks=depth,
    )
    held = [input_grads(slot) for slot in range(depth)]
    hops, held = phase(hops, held + [wides, *sides[0], *sides[1]])
    cat_grads, wides = held[:depth], held[depth]
    sides = [held[depth + 1 : depth + 4], held[depth + 4 :]]
    for k, tile_there in enumerate(hops):
        strip = join_cols(tile_there, pair_strip(tile_there), 1)
        wides = shifted(
            strip.reshape(1, strip_cells, mid), canvas_box, (row ^ (k + 1)) * tile_h, width,
            reverse=True, places=jnp.full((1,), k + 1, jnp.int32), out_blocks=depth, into=wides,
        )
    wides = wides.reshape(depth * strip_cells, 3 * mid)

    def weight_grads(kind):
        return jnp.stack(
            [
                dot(
                    sides[kind][a], wides[:, j * mid : (j + 1) * mid], contract_first
                ).astype(bf16)
                for a in range(3)
                for j in range(3)
            ]
        )

    away = ImageSum(weight_grads(0))
    sends, marker = mark(*away.first_sends())
    flights = away.first(sends)
    held = [input_grads(slot, marker) for slot in range(depth, row_count)]
    got, held = phase(flights, held + [own_means, wides])
    cat_grads += held[:-2]
    own_means, wides = held[-2:]
    flights = away.second(away.second_sends(got))
    by_row = [choose(cat_grads, row ^ r) for r in range(row_count)]
    spread_strip = lax.slice_in_dim(spread_ext, width, width + strip_cells, axis=1)
    grad_bins_local = jnp.zeros((branch_width, bins), f32)
    for r in range(feature_rows, row_count):
        first = (r * col_count + col) * block - channels_in
        keep = jnp.asarray(table[:, 0]) == lax.div(first, branch_width)
        terms = dot(by_row[r], spread_strip, (((0,), (1,)), ((), ())))
        terms = jnp.where(keep[None], terms, 0.0)
        at = lax.rem(first, branch_width)
        old = lax.dynamic_slice_in_dim(grad_bins_local, at, block, 0)
        grad_bins_local = lax.dynamic_update_slice_in_dim(grad_bins_local, old + terms, at, 0)
    wides, grad_bins_local = tie(wides, grad_bins_local)
    got, (home,) = phase(flights, [weight_grads(1)])
    home = ImageSum(home)
    crossing = [swap(jnp.concatenate(away.reduced(got), axis=1), "row", depth)]
    grad_bins = lax.psum_scatter(
        grad_bins_local, ("row", "col"), scatter_dimension=0, tiled=True
    )
    grad_act = grad_bins * silu_slope(before)
    branch_sums = butterfly(
        jnp.concatenate([by_scale(grad_act * normed), by_scale(grad_act)], axis=0), ("img",)
    )
    got, (branch_sums,) = phase(home.first(home.first_sends()), [branch_sums])
    sends, second_mark = mark(*home.second_sends(got))
    flights = home.second(sends)
    grad_pre = (
        gain_part
        * inverse_bins
        * (
            grad_act
            - to_bins(branch_sums[4:] / counts)
            - normed * to_bins(branch_sums[:4] / counts)
        )
    ).astype(bf16)
    got, _ = phase(flights + crossing)
    home_own = home.reduced(got[:2])
    crossed = [got[2][:, : home.half], got[2][:, home.half :]]
    home_own = [add_low(a, b) for a, b in zip(home_own, crossed)]
    got, _ = phase(home.third(home_own))
    sends, fourth_mark = mark(*home.fourth_sends(got))
    got = home.fourth(sends)
    while class_chain.todo:
        phase([])
    class_w_grad, class_bias_grad = class_chain.value[:mid], class_chain.value[mid]
    gathered = lax.all_gather(
        jnp.concatenate([grad_pre.astype(f32), branch_sums.T], axis=1) + second_mark[0, 0],
        ("row", "col"), axis=0, tiled=True,
    )
    grad_pre = gathered[:, :bins].astype(bf16)
    branch_all = gathered[:, bins:].T
    branch_gain_grad, branch_bias_grad = branch_all[:4], branch_all[4:]

    late_pre = (gathered[:, :bins] + fourth_mark[0, 0]).astype(bf16)
    weight_terms, bin_grads = [], []
    for position in range(4):
        span = slice(limits[position], limits[position + 1])
        weight_terms.append(
            dot(own_means[span], grad_pre[:, span], (((0,), (1,)), ((), ())))
        )
        bin_grads.append(
            dot(
                late_pre[:, span], branch_projection_weight[position], (((0,), (1,)), ((), ()))
            )
        )
    bin_grads = (jnp.concatenate(bin_grads, axis=0) / sizes[:, None]).astype(bf16)
    grad_pool = dot(pooling, bin_grads, contract_first)

    own_features = [
        by_row[r].reshape(tile_h, width, block) for r in range(feature_rows)
    ]

    def feature_grads_of(step):
        return jnp.stack(
            [
                choose(
                    [one[:, c * tile_w : (c + 1) * tile_w] for c in range(col_count)], col ^ step
                ).reshape(pixels, block)
                for one in own_features
            ]
        )

    by_step = [feature_grads_of(0)] + [
        swap(feature_grads_of(step), "col", step) for step in range(1, col_count)
    ]
    by_block = [choose(by_step, col ^ c) for c in range(col_count)]
    joined = jnp.concatenate(
        [by_block[c][r] for r in range(feature_rows) for c in range(col_count)], axis=1
    )
    feature_grad = (joined.astype(f32) + grad_pool).reshape(1, tile_h, tile_w, channels_in)

    branch_w_grad = lax.psum(jnp.stack(weight_terms).astype(bf16), "img")
    branch_w_grad, *got = tie(branch_w_grad, *got)
    branch_w_grad = branch_w_grad.astype(f32)
    conv_w_grad = home.gathered(got)
    conv_w_grad = jnp.transpose(conv_w_grad, (1, 0, 2))
    return (
        logits.reshape(1, tile_h, tile_w, classes),
        feature_grad,
        branch_w_grad,
        branch_gain_grad,
        branch_bias_grad,
        conv_w_grad,
        conv_gain_grad,
        conv_bias_grad,
        class_w_grad,
        class_bias_grad,
    )


def solution(mesh):
    return jax.shard_map(
        on_device,
        mesh=mesh,
        in_specs=(
            P("img", "row", "col", None),
            P("img", None, None),
            P("img", "row", "col"),
            P(),
            P(),
            P(),
            P(("row", "col"), None, None),
            P(),
            P(),
            P(),
            P(),
        ),
        out_specs=(
            P("img", "row", "col", None),
            P("img", "row", "col", None),
            P(None, ("row", "col"), None),
            P(),
            P(),
            P(("row", "col"), None, None),
            P(),
            P(),
            P(),
            P(),
        ),
        check_vma=False,
    )
```

```python
import jax
import jax.numpy as jnp
import numpy as np
from jax import lax
from jax.experimental import pallas as pl
from jax.experimental.pallas import tpu as pltpu
from jax.sharding import PartitionSpec as P

bin_scales = (1, 2, 3, 6)
norm_eps = 1e-05
tap_offsets = ((-1, -1), (-1, 0), (-1, 1), (0, -1), (0, 0), (0, 1), (1, -1), (1, 0), (1, 1))
contract_first = (((0,), (0,)), ((), ()))
contract_last = (((1,), (1,)), ((), ()))
bf16 = jnp.bfloat16
f32 = jnp.float32


def dot(a, b, dims=(((1,), (0,)), ((), ()))):
    return lax.dot_general(a, b, dims, preferred_element_type=f32)


def swap(value, axis, step):
    count = lax.axis_size(axis)
    return lax.ppermute(value, axis, [(i, i ^ step) for i in range(count)])


def butterfly(value, axes):
    for axis in axes:
        step = 1
        while step < lax.axis_size(axis):
            value = value + swap(value, axis, step)
            step *= 2
    return value


def bin_constants(regions):
    rows = []
    for position, scale in enumerate(bin_scales):
        for r in range(regions):
            for i in range(scale):
                for j in range(scale):
                    rows.append((position, scale, r, i, j))
    return np.asarray(rows, np.int32)


def of_bin_boxes(canvas_box, table):
    pick = jnp.asarray(table[:, 2:3] == np.arange(canvas_box.shape[0])[None, :], jnp.int32)
    return jnp.sum(pick[:, :, None] * canvas_box[None], axis=1)


def members(edges, cells_y, cells_x):
    lo_y, hi_y, lo_x, hi_x = (edge[:, None] for edge in edges)
    y, x = cells_y[None, :], cells_x[None, :]
    return ((y >= lo_y) & (y < hi_y) & (x >= lo_x) & (x < hi_x)).astype(bf16)


def axis_weight(cells, first, last, scale, index):
    extent = (last - first - 1).astype(f32)[:, None]
    place = ((cells[None, :] - first[:, None]) * (scale - 1)[:, None]).astype(f32)
    away = jnp.abs(place - index.astype(f32)[:, None] * extent) / extent
    inside = (cells[None, :] >= first[:, None]) & (cells[None, :] < last[:, None])
    return jnp.where(inside, jnp.maximum(1.0 - away, 0.0), 0.0)


def spreads(boxes, table, cells_y, cells_x):
    scale, i, j = (jnp.asarray(table[:, k]) for k in (1, 3, 4))
    weight_y = axis_weight(cells_y, boxes[:, 0], boxes[:, 2], scale, i)
    weight_x = axis_weight(cells_x, boxes[:, 1], boxes[:, 3], scale, j)
    return (weight_y * weight_x).astype(bf16)


def grid_cells(rows, cols):
    y = jnp.broadcast_to(rows[:, None], (rows.shape[0], cols.shape[0])).reshape(-1)
    x = jnp.broadcast_to(cols[None, :], (rows.shape[0], cols.shape[0])).reshape(-1)
    return y, x


def row_masks(canvas_box, rows, cols):
    y, x = rows[:, None], cols[None, :]
    up, left, down, right = (canvas_box[:, k][:, None, None] for k in range(4))
    inside = (y >= up) & (y < down) & (x >= left) & (x < right)
    upper = jnp.any(inside & (y > up), axis=0)
    lower = jnp.any(inside & (y + 1 < down), axis=0)
    return upper.reshape(-1), lower.reshape(-1)


small_cost = pl.CostEstimate(flops=1024, bytes_accessed=1024, transcendentals=0)


def shift_lines(box_ref, first, x_ref, o_ref, width, reverse):
    cells, block = x_ref.shape
    order = (2, 1, 0) if reverse else (0, 1, 2)
    left_at, mid_at, right_at = (place * block for place in order)

    def line(at, carry):
        y = first + at
        here = pl.ds(pl.multiple_of(at * width, width), width)
        x = lax.broadcasted_iota(jnp.int32, (width, block), 0)
        no_left = x == 0
        no_right = x == width - 1
        for r in range(box_ref.shape[0]):
            inside = (y >= box_ref[r, 0]) & (y < box_ref[r, 2])
            no_left = no_left | (x == jnp.where(inside, box_ref[r, 1], -1))
            no_right = no_right | (x == jnp.where(inside, box_ref[r, 3] - 1, -1))
        own = x_ref[here, :]
        wide = own.astype(f32)
        left = jnp.where(no_left, 0.0, pltpu.roll(wide, 1, 0))
        right = jnp.where(no_right, 0.0, pltpu.roll(wide, width - 1, 0))
        o_ref[here, left_at : left_at + block] = left.astype(bf16)
        o_ref[here, mid_at : mid_at + block] = own
        o_ref[here, right_at : right_at + block] = right.astype(bf16)
        return carry

    lax.fori_loop(0, cells // width, line, 0)


def shifted(x, canvas_box, first_line, width, reverse=False, places=None, out_blocks=1, into=None):
    blocks, cells, block = x.shape
    total = cells // width
    lines = max(k for k in range(1, total + 1) if total % k == 0 and k * width <= 2048)
    if places is None:
        places, out_blocks = jnp.arange(blocks, dtype=jnp.int32), blocks

    def body(place_ref, first_ref, box_ref, x_ref, *rest):
        first = first_ref[0] + pl.program_id(1) * lines
        shift_lines(box_ref, first, x_ref.at[0], rest[-1].at[0], width, reverse)

    extra = [] if into is None else [into]
    return pl.pallas_call(
        body,
        grid_spec=pltpu.PrefetchScalarGridSpec(
            num_scalar_prefetch=2,
            grid=(blocks, total // lines),
            in_specs=[
                pl.BlockSpec(memory_space=pltpu.SMEM),
                pl.BlockSpec((1, width * lines, block), lambda b, i, at, first: (b, i, 0)),
            ]
            + [pl.BlockSpec(memory_space=pl.ANY)] * len(extra),
            out_specs=pl.BlockSpec(
                (1, width * lines, 3 * block), lambda b, i, at, first: (at[b], i, 0)
            ),
        ),
        out_shape=jax.ShapeDtypeStruct((out_blocks, cells, 3 * block), bf16),
        input_output_aliases={4: 0} if extra else {},
        compiler_params=pltpu.CompilerParams(vmem_limit_bytes=52 << 20),
        cost_estimate=small_cost,
    )(places, jnp.reshape(first_line, (1,)).astype(jnp.int32), canvas_box, x, *extra)


def chunk_of(cells, width):
    total = cells // width
    return max(k for k in range(1, total + 1) if total % k == 0 and k * width <= 1024) * width


def conv_slot(wide, slot, weight, keeps, total, width):
    _, ext, deep = wide.shape
    _, block, mid = weight[0].shape
    cells = keeps.shape[1]
    chunk = chunk_of(cells, width)

    def body(x_ref, *rest):
        w_refs, keep_ref, o_ref = rest[:3], rest[3], rest[-1]
        begin = pl.program_id(0) * chunk
        value = 0.0 if total is None else rest[4][...]
        for a in range(3):
            term = jnp.dot(
                x_ref[0, pl.ds(pl.multiple_of(begin + a * width, width), chunk), :],
                w_refs[a][...].reshape(3 * block, mid),
                preferred_element_type=f32,
            )
            value = value + (term if a == 1 else keep_ref[a] * term)
        o_ref[...] = value

    extra = [] if total is None else [total]
    once = pl.Buffered(1)
    one = pl.BlockSpec((3, block, mid), lambda c: (0, 0, 0), pipeline_mode=once)
    return pl.pallas_call(
        body,
        grid=(cells // chunk,),
        in_specs=[
            pl.BlockSpec((1, ext, deep), lambda c: (slot, 0, 0), pipeline_mode=once),
            one, one, one,
            pl.BlockSpec((3, chunk, 1), lambda c: (0, c, 0)),
        ]
        + [pl.BlockSpec((chunk, mid), lambda c: (c, 0))] * len(extra),
        out_specs=pl.BlockSpec((chunk, mid), lambda c: (c, 0)),
        out_shape=jax.ShapeDtypeStruct((cells, mid), f32),
        input_output_aliases={5: 0} if extra else {},
        compiler_params=pltpu.CompilerParams(vmem_limit_bytes=32 << 20),
        cost_estimate=small_cost,
    )(wide, *weight, keeps, *extra)


def grad_slot(wide, weight, keeps, width, marker=None):
    ext, deep = wide.shape
    _, block, mid = weight[0].shape
    cells = keeps.shape[1]
    chunk = chunk_of(cells, width)

    def body(x_ref, *rest):
        w_refs, keep_ref, o_ref = rest[:3], rest[3], rest[-1]
        begin = pl.program_id(0) * chunk
        value = 0.0
        for a in range(3):
            rows = pl.ds(pl.multiple_of(begin + a * width, width), chunk)
            term = 0.0
            for j in range(3):
                term = term + lax.dot_general(
                    x_ref[rows, j * mid : (j + 1) * mid],
                    w_refs[2 - a][j],
                    contract_last,
                    preferred_element_type=f32,
                )
            value = value + (term if a == 1 else keep_ref[a] * term)
        o_ref[...] = value.astype(bf16)

    extra = [] if marker is None else [marker]
    once = pl.Buffered(1)
    one = pl.BlockSpec((3, block, mid), lambda c: (0, 0, 0), pipeline_mode=once)
    return pl.pallas_call(
        body,
        grid=(cells // chunk,),
        in_specs=[
            pl.BlockSpec((ext, deep), lambda c: (0, 0), pipeline_mode=once),
            one, one, one,
            pl.BlockSpec((3, chunk, 1), lambda c: (0, c, 0)),
        ]
        + [pl.BlockSpec(memory_space=pl.ANY)] * len(extra),
        out_specs=pl.BlockSpec((chunk, block), lambda c: (c, 0)),
        out_shape=jax.ShapeDtypeStruct((cells, block), bf16),
        compiler_params=pltpu.CompilerParams(vmem_limit_bytes=32 << 20),
        cost_estimate=small_cost,
    )(wide, *weight, keeps, *extra)


def weight_slot(sides, wides, marker=None):
    _, cells, block = sides.shape
    mid = wides.shape[1] // 3

    def body(side_ref, wide_ref, *rest):
        o_ref = rest[-1]
        terms = lax.dot_general(
            side_ref[0], wide_ref[...], contract_first, preferred_element_type=f32
        )
        for j in range(3):
            o_ref[j] = terms[:, j * mid : (j + 1) * mid].astype(bf16)

    extra = [] if marker is None else [marker]
    return pl.pallas_call(
        body,
        grid=(3,),
        in_specs=[
            pl.BlockSpec((1, cells, block), lambda a: (a, 0, 0)),
            pl.BlockSpec((cells, 3 * mid), lambda a: (0, 0), pipeline_mode=pl.Buffered(1)),
        ]
        + [pl.BlockSpec(memory_space=pl.ANY)] * len(extra),
        out_specs=pl.BlockSpec((3, block, mid), lambda a: (a, 0, 0)),
        out_shape=jax.ShapeDtypeStruct((9, block, mid), bf16),
        compiler_params=pltpu.CompilerParams(vmem_limit_bytes=52 << 20),
        cost_estimate=small_cost,
    )(sides, wides, *extra)


def weight_sums(sides, wides, marker=None):
    _, cells, _ = sides.shape
    mid = wides.shape[1] // 3
    if cells * mid <= 3072 * 512:
        return weight_slot(sides, wides, marker)
    return jnp.stack(
        [
            dot(sides[a], wides[:, j * mid : (j + 1) * mid], contract_first).astype(bf16)
            for a in range(3)
            for j in range(3)
        ]
    )


def pool_back(grads, projections, limits, shares, pooled, joined):
    scales, wide, deep = projections.shape
    cells, bins = pooled.shape
    _, more = grads.shape
    block = wide // 4

    def body(grad_ref, w_ref, share_ref, pool_ref, join_ref, o_ref):
        lane = lax.broadcasted_iota(jnp.int32, (deep, more), 1)
        grad = grad_ref[...].astype(f32)
        total = 0.0
        for s in range(scales):
            inside = (lane >= limits[s]) & (lane < limits[s + 1])
            part = jnp.where(inside, grad, 0.0).astype(bf16)
            total = total + jnp.dot(w_ref[s], part, preferred_element_type=f32)
        value = (total[:, :bins] * share_ref[...]).astype(bf16)
        o_ref[...] = join_ref[...].astype(f32) + lax.dot_general(
            pool_ref[...], value, contract_last, preferred_element_type=f32
        )

    return pl.pallas_call(
        body,
        grid=(4,),
        in_specs=[
            pl.BlockSpec((deep, more), lambda c: (0, 0)),
            pl.BlockSpec((scales, block, deep), lambda c: (0, c, 0)),
            pl.BlockSpec((1, bins), lambda c: (0, 0)),
            pl.BlockSpec((cells, bins), lambda c: (0, 0)),
            pl.BlockSpec((cells, block), lambda c: (0, c)),
        ],
        out_specs=pl.BlockSpec((cells, block), lambda c: (0, c)),
        out_shape=jax.ShapeDtypeStruct((cells, wide), f32),
        compiler_params=pltpu.CompilerParams(vmem_limit_bytes=40 << 20),
        cost_estimate=small_cost,
    )(grads, projections, shares, pooled, joined)


def silu_slope(value):
    sigmoid_value = jax.nn.sigmoid(value)
    return sigmoid_value * (1.0 + value * (1.0 - sigmoid_value))


def choose(options, index):
    value = options[0]
    for k in range(1, len(options)):
        value = jnp.where(index == k, options[k], value)
    return value


def table_at(values, index):
    return choose([jnp.int32(value) for value in values], index)


def tie(*arrays):
    return list(lax.optimization_barrier(tuple(arrays)))


class Rows:
    def __init__(self, own):
        self.count = lax.axis_size("row")
        self.row = lax.axis_index("row")
        self.right = self.left = own
        self.arrived = {}
        self.step = 0

    def kinds(self, k):
        return [(abs(z - (z ^ k)), int((z ^ k) > z)) for z in range(self.count)]

    def more(self):
        return self.step < self.count - 1

    def send(self):
        self.step += 1
        step, count = self.step, self.count
        to_right = [(z, z + 1) for z in range(step - 1, count - 1)]
        to_left = [(z, z - 1) for z in range(1, count - step + 1)]
        return [
            lax.ppermute(self.right, "row", to_right),
            lax.ppermute(self.left, "row", to_left),
        ]

    def receive(self, results):
        self.right, self.left = results[0], results[-1]
        self.arrived[self.step] = (self.right, self.left)

    def ready(self, k):
        return max(step for step, _ in self.kinds(k)) <= self.step

    def slot(self, k):
        each = self.kinds(k)
        options = sorted(set(each))
        which = table_at([options.index(kind) for kind in each], self.row)
        return choose([self.arrived[step][side] for step, side in options], which)


def place_images(pieces, kind=bf16):
    me = lax.axis_index("img")
    first = pieces[0]
    width = first.shape[1]
    shape = (first.shape[0], len(pieces) * width) + first.shape[2:]
    joined = jnp.zeros(shape, kind)
    for step, piece in enumerate(pieces):
        joined = lax.dynamic_update_slice_in_dim(
            joined, piece.astype(kind), (me ^ step) * width, 1
        )
    return joined


class Chain:
    def __init__(self, value, axes):
        self.value = value
        self.todo = []
        for axis in axes:
            step = 1
            while step < lax.axis_size(axis):
                self.todo.append((axis, step))
                step *= 2

    def send(self):
        return [swap(self.value, *self.todo[0])] if self.todo else []

    def receive(self, got):
        if got:
            self.value = self.value + got[0]
            self.todo = self.todo[1:]


def mark(*arrays):
    tiny = jnp.zeros((8, 128), f32)
    *arrays, tiny = tie(*arrays, tiny)
    return arrays, swap(tiny, "col", 1)


def add_low(a, b):
    return (a.astype(f32) + b.astype(f32)).astype(bf16)


class ImageSum:
    def __init__(self, x):
        self.x = x
        self.me = lax.axis_index("img")
        self.half = x.shape[1] // 8

    def piece(self, j, side):
        at = (self.me ^ j) * 2 * self.half + side * self.half
        return lax.dynamic_slice_in_dim(self.x, at, self.half, 1)

    def first_sends(self):
        return [
            jnp.concatenate([self.piece(1, 0), self.piece(3, 0)], axis=1),
            jnp.concatenate([self.piece(2, 1), self.piece(3, 1)], axis=1),
        ]

    def first(self, sends):
        return [swap(sends[0], "img", 1), swap(sends[1], "img", 2)]

    def second_sends(self, got):
        half = self.half
        self.own = [add_low(self.piece(0, k), got[k][:, :half]) for k in range(2)]
        return [
            add_low(self.piece(2, 0), got[0][:, half:]),
            add_low(self.piece(1, 1), got[1][:, half:]),
        ]

    def second(self, sends):
        return [swap(sends[0], "img", 2), swap(sends[1], "img", 1)]

    def reduced(self, got):
        self.own = [add_low(a, b) for a, b in zip(self.own, got)]
        return self.own

    def third(self, own):
        self.own = own
        return [swap(own[0], "img", 1), swap(own[1], "img", 2)]

    def fourth_sends(self, got):
        self.next = got
        return [jnp.concatenate([own, near], axis=1) for own, near in zip(self.own, got)]

    def fourth(self, sends):
        return [swap(sends[0], "img", 2), swap(sends[1], "img", 1)]

    def gathered(self, got):
        half = self.half
        own, near = self.own, self.next
        parts = [
            (0, 0, own[0]),
            (0, 1, own[1]),
            (1, 0, near[0]),
            (2, 1, near[1]),
            (2, 0, got[0][:, :half]),
            (3, 0, got[0][:, half:]),
            (1, 1, got[1][:, :half]),
            (3, 1, got[1][:, half:]),
        ]
        taps, _, mid = self.x.shape
        whole = jnp.zeros((taps, 8 * half, mid), f32)
        for j, side, part in parts:
            at = (self.me ^ j) * 2 * half + side * half
            whole = lax.dynamic_update_slice_in_dim(whole, part.astype(f32), at, 1)
        return whole


def join_cols(mine, others, axis):
    col = lax.axis_index("col")
    pieces = [mine] + list(others)
    return jnp.concatenate([choose(pieces, col ^ c) for c in range(len(pieces))], axis=axis)


def row_halo(lines):
    count = lax.axis_size("row")
    above = lax.ppermute(lines[-1:], "row", [(i, i + 1) for i in range(count - 1)])
    below = lax.ppermute(lines[:1], "row", [(i + 1, i) for i in range(count - 1)])
    return jnp.concatenate([above, lines, below], axis=0)


def on_device(
    features,
    region_boxes,
    labels,
    branch_projection_weight,
    branch_gain,
    branch_bias,
    conv_w,
    conv_gain,
    conv_bias,
    class_w,
    class_bias,
):
    _, tile_h, tile_w, channels_in = features.shape
    pixels = tile_h * tile_w
    images, row_count, col_count = (lax.axis_size(axis) for axis in ("img", "row", "col"))
    img, row, col = (lax.axis_index(axis) for axis in ("img", "row", "col"))
    groups = row_count * col_count
    block, taps, mid = conv_w.shape
    branch_width = branch_projection_weight.shape[2]
    feature_rows = channels_in // (block * col_count)
    regions = region_boxes.shape[1]
    height, width = row_count * tile_h, col_count * tile_w
    all_cells = images * height * width
    canvas_box = region_boxes[0]
    table = bin_constants(regions)
    bins = table.shape[0]
    limits = [0]
    for scale in bin_scales:
        limits.append(limits[-1] + regions * scale * scale)
    scale_rows = [
        jnp.asarray((table[:, 0] == position).astype(np.float32)) for position in range(4)
    ]

    weight = jnp.transpose(conv_w, (1, 0, 2))
    share = block // images
    own_share, tile = tie(
        lax.dynamic_slice_in_dim(weight, img * share, share, 1),
        features[0].reshape(pixels, channels_in),
    )
    rows = Rows(own_share)

    def by_line(nine):
        return [nine[3 * a : 3 * a + 3] for a in range(3)]

    weights = [by_line(weight)]
    waiting = {"next": 1, "send": [], "plan": [], "slot": None, "place": []}

    def weight_plan(before=()):
        plan, send = [], [[], []]
        if waiting["slot"] is not None:
            pieces = waiting["slot"]
            half = share // 2
            send[0].append(pieces[2][:, half:])
            send[1].append(pieces[1][:, :half])
            plan.append(("close", pieces))
        if waiting["next"] < row_count and rows.ready(waiting["next"]):
            part = rows.slot(waiting["next"])
            waiting["next"] += 1
            send[0].append(part)
            send[1].append(part)
            plan.append(("cross", part))
        send = [jnp.concatenate(arrays, axis=1) for arrays in send if arrays]
        placed = waiting["place"] if plan else []
        got, waiting["mark"] = mark(*send, *before, *placed)
        waiting["send"], waiting["plan"] = got[: len(send)], plan
        end = len(got) - len(placed)
        place_now(got[end:] if plan else waiting["place"])
        return got[len(send) : end]

    def lines_of(pieces):
        return [place_images([piece[3 * a : 3 * a + 3] for piece in pieces]) for a in range(3)]

    def place_now(pieces):
        if pieces:
            weights.append(lines_of(pieces))
        waiting["place"] = []

    def weight_phase(more=(), hold=()):
        flights = [swap(send, "img", k + 1) for k, send in enumerate(waiting["send"])]
        count = len(flights)
        hop = waiting["hop"]
        flights += hop
        got = tie(*flights, *more, *hold)
        if hop:
            rows.receive(got[count : len(flights)])
        waiting["hop"] = rows.send() if rows.more() else []
        waiting["slot"] = None
        at = 0
        for what, kept in waiting["plan"]:
            size = share // 2 if what == "close" else share
            part = [array[:, at : at + size] for array in got[:count]]
            at += size
            if what == "close":
                far = jnp.concatenate([part[1], part[0]], axis=1)
                waiting["place"] = kept + [far]
            else:
                waiting["slot"] = [kept] + part
        at = len(flights)
        return got[at : at + len(more)], got[at + len(more) :]

    waiting["hop"] = rows.send()

    tile_ext = row_halo(tile.reshape(tile_h, tile_w, channels_in))

    def channels_of(c):
        at = [(r * col_count + c) * block for r in range(feature_rows)]
        return jnp.stack([tile_ext[..., k : k + block] for k in at])

    by_col = [channels_of(c) for c in range(col_count)]
    sent = [choose(by_col, col ^ step) for step in range(col_count)]
    strip_ext = join_cols(
        sent[0], [swap(sent[step], "col", step) for step in range(1, col_count)], 2
    )
    weight_phase()
    (strip_ext,) = weight_plan([strip_ext])

    boxes = of_bin_boxes(canvas_box, table)
    scale, bin_i, bin_j = (jnp.asarray(table[:, k]) for k in (1, 3, 4))
    extent_y, extent_x = boxes[:, 2] - boxes[:, 0], boxes[:, 3] - boxes[:, 1]
    edges = (
        boxes[:, 0] + lax.div(bin_i * extent_y, scale),
        boxes[:, 0] + lax.div((bin_i + 1) * extent_y + scale - 1, scale),
        boxes[:, 1] + lax.div(bin_j * extent_x, scale),
        boxes[:, 1] + lax.div((bin_j + 1) * extent_x + scale - 1, scale),
    )
    sizes = ((edges[1] - edges[0]) * (edges[3] - edges[2])).astype(f32)
    top, left = row * tile_h, col * tile_w
    tile_y, tile_x = grid_cells(
        top + jnp.arange(tile_h, dtype=jnp.int32), left + jnp.arange(tile_w, dtype=jnp.int32)
    )
    pooling = members(edges, tile_y, tile_x)
    local_means = dot(pooling, tile) / sizes[:, None]
    local_low = local_means.astype(bf16)
    pre_local = jnp.concatenate(
        [
            dot(
                branch_projection_weight[position],
                local_low[limits[position] : limits[position + 1]],
                (((0,), (1,)), ((), ())),
            )
            for position in range(4)
        ],
        axis=1,
    )
    pre = lax.psum_scatter(pre_local, ("row", "col"), scatter_dimension=0, tiled=True)
    cat_blocks = strip_ext.reshape(feature_rows, -1, block)
    slots_of = row ^ jnp.arange(row_count, dtype=jnp.int32)
    cat_wide = shifted(
        cat_blocks, canvas_box, top - 1, width, places=slots_of[:feature_rows],
        out_blocks=row_count,
    )
    _, (pre, cat_wide) = weight_phase(hold=[pre, cat_wide])
    part = branch_width // groups
    group = row * col_count + col

    def by_scale(value):
        return jnp.stack([jnp.sum(value * line[None], axis=1) for line in scale_rows])

    def to_bins(value):
        return sum(value[k][:, None] * scale_rows[k][None] for k in range(4))

    def branch_part(value):
        return to_bins(lax.dynamic_slice_in_dim(value, group * part, part, 1))

    counts = np.asarray([images * regions * s * s for s in bin_scales], np.float32)[:, None]
    moments = butterfly(jnp.concatenate([by_scale(pre), by_scale(pre * pre)], axis=0), ("img",))
    moments, cat_wide = weight_plan([moments, cat_wide])
    center = moments[:4] / counts
    inverse = lax.rsqrt(moments[4:] / counts - center * center + norm_eps)
    gain_part = branch_part(branch_gain)
    inverse_bins = to_bins(inverse)
    normed = (pre - to_bins(center)) * inverse_bins
    before = gain_part * normed + branch_part(branch_bias)
    act_branch = lax.all_gather(
        (jax.nn.silu(before) + waiting["mark"][0, 0]).astype(bf16),
        ("row", "col"), axis=0, tiled=True,
    )

    def block_rows_of(r):
        first = (r * col_count + col) * block - channels_in
        position = lax.div(first, branch_width)
        taken = lax.dynamic_slice_in_dim(
            act_branch, jnp.maximum(lax.rem(first, branch_width), 0), block, 0
        )
        keep = jnp.asarray(table[:, 0]) == position
        return jnp.where(keep[None], taken, jnp.zeros((), bf16)), keep

    strip_cols = jnp.arange(width, dtype=jnp.int32)
    strip_cells = tile_h * width
    ext_cells = strip_cells + 2 * width

    def ext_spread(source):
        lines = source * tile_h - 1 + jnp.arange(tile_h + 2, dtype=jnp.int32)
        return spreads(boxes, table, *grid_cells(lines, strip_cols))

    def up_blocks(spread, r):
        return dot(spread, block_rows_of(r)[0], (((0,), (1,)), ((), ()))).astype(bf16)

    spread_ext = ext_spread(row)
    ups = jnp.stack([up_blocks(spread_ext, r) for r in range(feature_rows, row_count)])
    cat_wide = shifted(
        ups, canvas_box, top - 1, width, places=slots_of[feature_rows:],
        out_blocks=row_count, into=cat_wide,
    )
    upper, lower = row_masks(canvas_box, jnp.arange(height, dtype=jnp.int32), strip_cols)

    def strip_of(cells, source):
        return lax.dynamic_slice_in_dim(cells, source * strip_cells, strip_cells, 0)

    keeps = jnp.stack(
        [strip_of(upper, row), jnp.ones((strip_cells,), bool), strip_of(lower, row)]
    ).astype(f32)[:, :, None]

    depth = row_count // 2
    place = lax.rem(row, depth)
    _, (cat_wide, cat_blocks) = weight_phase(hold=[cat_wide, cat_blocks])

    def moved(step):
        return lax.dynamic_index_in_dim(cat_blocks, place ^ step, 0, keepdims=False)

    own_ext, *sends, cat_wide = weight_plan([moved(step) for step in range(depth)] + [cat_wide])
    feature_exts = {0: own_ext}
    hidden_strip = conv_slot(cat_wide, 0, weights[0], keeps, None, width)
    for slot in range(1, row_count):
        while len(weights) <= slot:
            step = len(feature_exts)
            more = [swap(sends[step - 1], "row", step)] if step < depth else []
            got, hold = weight_phase(more=more, hold=[hidden_strip])
            if got:
                feature_exts[step] = got[0]
            if len(weights) == row_count - 2:
                hidden_strip, mean_moves = weight_plan(hold + [local_means.astype(bf16)])
            else:
                (hidden_strip,) = weight_plan(hold)
        hidden_strip = conv_slot(cat_wide, slot, weights[slot], keeps, hidden_strip, width)
    for step in range(1, depth):
        if step not in feature_exts:
            feature_exts[step] = swap(sends[step - 1], "row", step)
    own_means = lax.psum_scatter(mean_moves, ("row", "col"), scatter_dimension=1, tiled=True)
    hidden_strip = hidden_strip.reshape(tile_h, width, mid)

    def cells_of(step):
        return lax.dynamic_slice_in_dim(hidden_strip, (col ^ step) * tile_w, tile_w, 1)

    hidden = cells_of(0)
    for step in range(1, col_count):
        hidden = hidden + swap(cells_of(step), "col", step)
    hidden = hidden.reshape(pixels, mid)

    everywhere = ("col", "img", "row")
    mid_moments = butterfly(
        jnp.stack([jnp.sum(hidden, axis=0), jnp.sum(hidden * hidden, axis=0)]), everywhere
    )
    center_mid = mid_moments[0] / all_cells
    inverse_mid = lax.rsqrt(mid_moments[1] / all_cells - center_mid * center_mid + norm_eps)
    normed_mid = (hidden - center_mid) * inverse_mid
    before_mid = conv_gain * normed_mid + conv_bias
    act_mid = jax.nn.silu(before_mid).astype(bf16)
    logits = dot(act_mid, class_w) + class_bias
    classes = class_w.shape[1]
    onehot = (
        labels[0].reshape(pixels)[:, None] == jnp.arange(classes, dtype=jnp.int32)[None, :]
    ).astype(f32)
    grad_logits = (jax.nn.softmax(logits, axis=-1) - onehot).astype(bf16)
    grad_before = dot(grad_logits, class_w, contract_last) * silu_slope(before_mid)
    mid_grads = butterfly(
        jnp.stack([jnp.sum(grad_before * normed_mid, axis=0), jnp.sum(grad_before, axis=0)]),
        everywhere,
    )
    low_zero = jnp.zeros((), bf16)
    lower_half = row < depth
    up_exts = [choose([ups[r] for r in range(depth)], place)] + [
        up_blocks(ext_spread(row ^ step), feature_rows + place) for step in range(1, depth)
    ]
    exts = [
        (
            jnp.where(lower_half, up_exts[step], feature_exts[step]),
            jnp.where(lower_half, feature_exts[step], up_exts[step]),
        )
        for step in range(depth)
    ]
    sides = []
    for kind in range(2):
        lines = []
        for a in range(3):
            pieces = []
            for step in range(depth):
                piece = exts[step][kind][a * width : a * width + strip_cells]
                if a != 1:
                    keep = strip_of((upper, None, lower)[a], row ^ step)
                    piece = jnp.where(keep[:, None], piece, low_zero)
                pieces.append(piece)
            lines.append(jnp.concatenate(pieces, axis=0))
        sides.append(lines)

    mid_grads, home_side, *lines = tie(mid_grads, jnp.stack(sides[1]), *sides[0])
    sides = [lines]
    conv_gain_grad, conv_bias_grad = mid_grads[0], mid_grads[1]
    background = ("img", "row", "col")
    class_chain = Chain(
        jnp.concatenate(
            [
                dot(act_mid, grad_logits, contract_first),
                jnp.sum(grad_logits.astype(f32), axis=0, keepdims=True),
            ],
            axis=0,
        ),
        background,
    )
    grad_hidden = (
        conv_gain
        * inverse_mid
        * (grad_before - conv_bias_grad / all_cells - normed_mid * conv_gain_grad / all_cells)
    ).astype(bf16)

    def pair_strip(mine):
        return [swap(mine, "col", step) for step in range(1, col_count)]

    grad_tile = grad_hidden.reshape(tile_h, tile_w, mid)
    hops = [swap(grad_tile, "row", step) for step in range(1, depth)]
    grad_ext = row_halo(grad_tile)
    grad_ext = join_cols(grad_ext, pair_strip(grad_ext), 1)
    grad_strip = grad_ext[1:-1]
    grad_ext = grad_ext.reshape(1, ext_cells, mid)
    own_wide = shifted(grad_ext, canvas_box, top - 1, width, reverse=True)[0]

    def input_grads(slot, marker=None):
        return grad_slot(own_wide, weights[slot], keeps, width, marker)

    def phase(flights, hold=(), chain=True):
        sent = class_chain.send() if chain else []
        got = tie(*flights, *sent, *hold)
        class_chain.receive(got[len(flights) : len(flights) + len(sent)])
        return got[: len(flights)], got[len(flights) + len(sent) :]

    wides = shifted(
        grad_strip.reshape(1, strip_cells, mid), canvas_box, top, width, reverse=True,
        places=jnp.zeros((1,), jnp.int32), out_blocks=depth,
    )
    held = [input_grads(slot) for slot in range(depth)]
    hops += [swap(own_means, "img", 1), swap(own_means, "img", 2)]
    hops, held = phase(hops, held + [wides])
    *hops, means_one, means_two = hops
    cat_grads, wides = held[:depth], held[depth]
    for k, tile_there in enumerate(hops):
        strip = join_cols(tile_there, pair_strip(tile_there), 1)
        wides = shifted(
            strip.reshape(1, strip_cells, mid), canvas_box, (row ^ (k + 1)) * tile_h, width,
            reverse=True, places=jnp.full((1,), k + 1, jnp.int32), out_blocks=depth, into=wides,
        )
    wides = wides.reshape(depth * strip_cells, 3 * mid)

    def weight_grads(kind):
        return jnp.stack(
            [
                dot(
                    sides[kind][a], wides[:, j * mid : (j + 1) * mid], contract_first
                ).astype(bf16)
                for a in range(3)
                for j in range(3)
            ]
        )

    class_sent = class_chain.send()
    away = ImageSum(weight_grads(0))
    (*sends, class_got), marker = mark(*away.first_sends(), *class_sent)
    class_chain.receive([class_got])
    flights = away.first(sends)
    flights.append(swap(means_one, "img", 2))
    home = weight_sums(home_side, wides, marker)
    got, (home,) = phase(flights, [home])
    home = ImageSum(home)
    means = [own_means, means_one, means_two, got.pop()]
    sends, marker = mark(*away.second_sends(got))
    flights = away.second(sends)
    held = [input_grads(slot, marker) for slot in range(depth, row_count)]
    got, held = phase(flights, held)
    cat_grads += held
    *sends, far_own, far_next = tie(*home.first_sends(), *away.reduced(got))
    got, (far_next,) = phase(
        home.first(sends) + [swap(far_own, "row", depth)], [far_next]
    )
    crossed = [got.pop()]
    sends, second_mark = mark(*home.second_sends(got))
    flights = home.second(sends) + [swap(far_next, "row", depth)]
    by_row = [choose(cat_grads, row ^ r) for r in range(row_count)]
    spread_strip = lax.slice_in_dim(spread_ext, width, width + strip_cells, axis=1)
    grad_bins_local = jnp.zeros((branch_width, bins), f32)
    for r in range(feature_rows, row_count):
        first = (r * col_count + col) * block - channels_in
        keep = jnp.asarray(table[:, 0]) == lax.div(first, branch_width)
        terms = dot(by_row[r], spread_strip, (((0,), (1,)), ((), ())))
        terms = jnp.where(keep[None], terms, 0.0)
        at = lax.rem(first, branch_width)
        old = lax.dynamic_slice_in_dim(grad_bins_local, at, block, 0)
        grad_bins_local = lax.dynamic_update_slice_in_dim(grad_bins_local, old + terms, at, 0)
    grad_bins = lax.psum_scatter(
        grad_bins_local.astype(bf16), ("row", "col"), scatter_dimension=0, tiled=True
    ).astype(f32)
    grad_act = (grad_bins + second_mark[0, 0]) * silu_slope(before)
    branch_sums = butterfly(
        jnp.concatenate([by_scale(grad_act * normed), by_scale(grad_act)], axis=0), ("img",)
    )
    grad_pre = (
        gain_part
        * inverse_bins
        * (
            grad_act
            - to_bins(branch_sums[4:] / counts)
            - normed * to_bins(branch_sums[:4] / counts)
        )
    ).astype(bf16)
    own_features = [
        by_row[r].reshape(tile_h, width, block) for r in range(feature_rows)
    ]

    def feature_grads_of(step):
        return jnp.stack(
            [
                choose(
                    [one[:, c * tile_w : (c + 1) * tile_w] for c in range(col_count)], col ^ step
                ).reshape(pixels, block)
                for one in own_features
            ]
        )

    by_step = [feature_grads_of(0)] + [
        swap(feature_grads_of(step), "col", step) for step in range(1, col_count)
    ]
    by_block = [choose(by_step, col ^ c) for c in range(col_count)]
    joined = jnp.concatenate(
        [by_block[c][r] for r in range(feature_rows) for c in range(col_count)], axis=1
    )
    by_scales = jnp.asarray(table[:, 0][None, :] == np.arange(4)[:, None], bf16)
    means = [
        jnp.concatenate([part * line[:, None] for line in by_scales], axis=1) for part in means
    ]
    sums = branch_sums.T
    high = sums.astype(bf16)
    middle = (sums - high.astype(f32)).astype(bf16)
    low = (sums - high.astype(f32) - middle.astype(f32)).astype(bf16)
    piece = jnp.concatenate([grad_pre, high, middle, low], axis=1)
    flights += [swap(piece, "img", 1), swap(piece, "img", 2)]
    pooled = jnp.transpose(pooling)
    got, (joined, pooled, *means) = phase(flights, [joined, pooled, *means], chain=False)
    *got, piece_one, piece_two = got
    home_own = home.reduced(got[:2])
    crossed.append(got[2])
    home_own = [add_low(a, b) for a, b in zip(home_own, crossed)]
    got, _ = phase(home.third(home_own) + [swap(piece_one, "img", 2)])
    packed = jnp.stack([piece, piece_one, piece_two, got.pop()])
    sends = home.fourth_sends(got)
    sends, fourth_mark = mark(*sends, *home.own, *home.next)
    home.own, home.next = sends[2:4], sends[4:]
    got = home.fourth(sends)
    while class_chain.todo:
        phase([])
    class_w_grad, class_bias_grad = class_chain.value[:mid], class_chain.value[mid]
    gathered = lax.all_gather(
        packed + fourth_mark[0, 0].astype(bf16), ("row", "col"), axis=1, tiled=True
    )
    ends = gathered[0, :, bins:].astype(f32)
    branch_all = (ends[:, :8] + ends[:, 8:16] + ends[:, 16:]).T
    branch_gain_grad, branch_bias_grad = branch_all[:4], branch_all[4:]
    branch_w_grad = sum(
        dot(means[k], gathered[k, :, :bins], (((0,), (1,)), ((), ()))) for k in range(images)
    ).reshape(4, -1, branch_width)
    feature_grad = pool_back(
        gathered[0], branch_projection_weight, limits, 1.0 / sizes[None], pooled, joined
    ).reshape(1, tile_h, tile_w, channels_in)
    feature_grad, *got = tie(feature_grad, *got)
    conv_w_grad = home.gathered(got)
    conv_w_grad = jnp.transpose(conv_w_grad, (1, 0, 2))
    return (
        logits.reshape(1, tile_h, tile_w, classes),
        feature_grad,
        branch_w_grad,
        branch_gain_grad,
        branch_bias_grad,
        conv_w_grad,
        conv_gain_grad,
        conv_bias_grad,
        class_w_grad,
        class_bias_grad,
    )


def solution(mesh):
    return jax.shard_map(
        on_device,
        mesh=mesh,
        in_specs=(
            P("img", "row", "col", None),
            P("img", None, None),
            P("img", "row", "col"),
            P(),
            P(),
            P(),
            P(("row", "col"), None, None),
            P(),
            P(),
            P(),
            P(),
        ),
        out_specs=(
            P("img", "row", "col", None),
            P("img", "row", "col", None),
            P(None, ("row", "col"), None),
            P(),
            P(),
            P(("row", "col"), None, None),
            P(),
            P(),
            P(),
            P(),
        ),
        check_vma=False,
    )
```

```python
import jax
import jax.numpy as jnp
import numpy as np
from jax import lax
from jax.experimental import pallas as pl
from jax.experimental.pallas import tpu as pltpu
from jax.sharding import PartitionSpec as P

bin_scales = (1, 2, 3, 6)
norm_eps = 1e-05
tap_offsets = ((-1, -1), (-1, 0), (-1, 1), (0, -1), (0, 0), (0, 1), (1, -1), (1, 0), (1, 1))
contract_first = (((0,), (0,)), ((), ()))
contract_last = (((1,), (1,)), ((), ()))
bf16 = jnp.bfloat16
f32 = jnp.float32


def dot(a, b, dims=(((1,), (0,)), ((), ()))):
    return lax.dot_general(a, b, dims, preferred_element_type=f32)


def swap(value, axis, step):
    count = lax.axis_size(axis)
    return lax.ppermute(value, axis, [(i, i ^ step) for i in range(count)])


def butterfly(value, axes):
    for axis in axes:
        step = 1
        while step < lax.axis_size(axis):
            value = value + swap(value, axis, step)
            step *= 2
    return value


def bin_constants(regions):
    rows = []
    for position, scale in enumerate(bin_scales):
        for r in range(regions):
            for i in range(scale):
                for j in range(scale):
                    rows.append((position, scale, r, i, j))
    return np.asarray(rows, np.int32)


def of_bin_boxes(canvas_box, table):
    pick = jnp.asarray(table[:, 2:3] == np.arange(canvas_box.shape[0])[None, :], jnp.int32)
    return jnp.sum(pick[:, :, None] * canvas_box[None], axis=1)


def members(edges, cells_y, cells_x):
    lo_y, hi_y, lo_x, hi_x = (edge[:, None] for edge in edges)
    y, x = cells_y[None, :], cells_x[None, :]
    return ((y >= lo_y) & (y < hi_y) & (x >= lo_x) & (x < hi_x)).astype(bf16)


def axis_weight(cells, first, last, scale, index):
    extent = (last - first - 1).astype(f32)[:, None]
    place = ((cells[None, :] - first[:, None]) * (scale - 1)[:, None]).astype(f32)
    away = jnp.abs(place - index.astype(f32)[:, None] * extent) / extent
    inside = (cells[None, :] >= first[:, None]) & (cells[None, :] < last[:, None])
    return jnp.where(inside, jnp.maximum(1.0 - away, 0.0), 0.0)


def spreads(boxes, table, cells_y, cells_x):
    scale, i, j = (jnp.asarray(table[:, k]) for k in (1, 3, 4))
    weight_y = axis_weight(cells_y, boxes[:, 0], boxes[:, 2], scale, i)
    weight_x = axis_weight(cells_x, boxes[:, 1], boxes[:, 3], scale, j)
    return (weight_y * weight_x).astype(bf16)


def grid_cells(rows, cols):
    y = jnp.broadcast_to(rows[:, None], (rows.shape[0], cols.shape[0])).reshape(-1)
    x = jnp.broadcast_to(cols[None, :], (rows.shape[0], cols.shape[0])).reshape(-1)
    return y, x


def row_masks(canvas_box, rows, cols):
    y, x = rows[:, None], cols[None, :]
    up, left, down, right = (canvas_box[:, k][:, None, None] for k in range(4))
    inside = (y >= up) & (y < down) & (x >= left) & (x < right)
    upper = jnp.any(inside & (y > up), axis=0)
    lower = jnp.any(inside & (y + 1 < down), axis=0)
    return upper.reshape(-1), lower.reshape(-1)


small_cost = pl.CostEstimate(flops=1024, bytes_accessed=1024, transcendentals=0)


def shift_lines(box_ref, first, x_ref, o_ref, width, reverse):
    cells, block = x_ref.shape
    order = (2, 1, 0) if reverse else (0, 1, 2)
    left_at, mid_at, right_at = (place * block for place in order)

    def line(at, carry):
        y = first + at
        here = pl.ds(pl.multiple_of(at * width, width), width)
        x = lax.broadcasted_iota(jnp.int32, (width, block), 0)
        no_left = x == 0
        no_right = x == width - 1
        for r in range(box_ref.shape[0]):
            inside = (y >= box_ref[r, 0]) & (y < box_ref[r, 2])
            no_left = no_left | (x == jnp.where(inside, box_ref[r, 1], -1))
            no_right = no_right | (x == jnp.where(inside, box_ref[r, 3] - 1, -1))
        own = x_ref[here, :]
        wide = own.astype(f32)
        left = jnp.where(no_left, 0.0, pltpu.roll(wide, 1, 0))
        right = jnp.where(no_right, 0.0, pltpu.roll(wide, width - 1, 0))
        o_ref[here, left_at : left_at + block] = left.astype(bf16)
        o_ref[here, mid_at : mid_at + block] = own
        o_ref[here, right_at : right_at + block] = right.astype(bf16)
        return carry

    lax.fori_loop(0, cells // width, line, 0)


def shifted(x, canvas_box, first_line, width, reverse=False, places=None, out_blocks=1, into=None):
    blocks, cells, block = x.shape
    total = cells // width
    lines = max(k for k in range(1, total + 1) if total % k == 0 and k * width <= 2048)
    if places is None:
        places, out_blocks = jnp.arange(blocks, dtype=jnp.int32), blocks

    def body(place_ref, first_ref, box_ref, x_ref, *rest):
        first = first_ref[0] + pl.program_id(1) * lines
        shift_lines(box_ref, first, x_ref.at[0], rest[-1].at[0], width, reverse)

    extra = [] if into is None else [into]
    return pl.pallas_call(
        body,
        grid_spec=pltpu.PrefetchScalarGridSpec(
            num_scalar_prefetch=2,
            grid=(blocks, total // lines),
            in_specs=[
                pl.BlockSpec(memory_space=pltpu.SMEM),
                pl.BlockSpec((1, width * lines, block), lambda b, i, at, first: (b, i, 0)),
            ]
            + [pl.BlockSpec(memory_space=pl.ANY)] * len(extra),
            out_specs=pl.BlockSpec(
                (1, width * lines, 3 * block), lambda b, i, at, first: (at[b], i, 0)
            ),
        ),
        out_shape=jax.ShapeDtypeStruct((out_blocks, cells, 3 * block), bf16),
        input_output_aliases={4: 0} if extra else {},
        compiler_params=pltpu.CompilerParams(vmem_limit_bytes=52 << 20),
        cost_estimate=small_cost,
    )(places, jnp.reshape(first_line, (1,)).astype(jnp.int32), canvas_box, x, *extra)


def chunk_of(cells, width):
    total = cells // width
    return max(k for k in range(1, total + 1) if total % k == 0 and k * width <= 1024) * width


def conv_slot(wide, slot, weight, keeps, total, width):
    _, ext, deep = wide.shape
    _, block, mid = weight[0].shape
    cells = keeps.shape[1]
    chunk = chunk_of(cells, width)

    def body(x_ref, *rest):
        w_refs, keep_ref, o_ref = rest[:3], rest[3], rest[-1]
        begin = pl.program_id(0) * chunk
        value = 0.0 if total is None else rest[4][...]
        for a in range(3):
            term = jnp.dot(
                x_ref[0, pl.ds(pl.multiple_of(begin + a * width, width), chunk), :],
                w_refs[a][...].reshape(3 * block, mid),
                preferred_element_type=f32,
            )
            value = value + (term if a == 1 else keep_ref[a] * term)
        o_ref[...] = value

    extra = [] if total is None else [total]
    once = pl.Buffered(1)
    one = pl.BlockSpec((3, block, mid), lambda c: (0, 0, 0), pipeline_mode=once)
    return pl.pallas_call(
        body,
        grid=(cells // chunk,),
        in_specs=[
            pl.BlockSpec((1, ext, deep), lambda c: (slot, 0, 0), pipeline_mode=once),
            one, one, one,
            pl.BlockSpec((3, chunk, 1), lambda c: (0, c, 0)),
        ]
        + [pl.BlockSpec((chunk, mid), lambda c: (c, 0))] * len(extra),
        out_specs=pl.BlockSpec((chunk, mid), lambda c: (c, 0)),
        out_shape=jax.ShapeDtypeStruct((cells, mid), f32),
        input_output_aliases={5: 0} if extra else {},
        compiler_params=pltpu.CompilerParams(vmem_limit_bytes=32 << 20),
        cost_estimate=small_cost,
    )(wide, *weight, keeps, *extra)


def grad_slot(wide, weight, keeps, width, marker=None):
    ext, deep = wide.shape
    _, block, mid = weight[0].shape
    cells = keeps.shape[1]
    chunk = chunk_of(cells, width)

    def body(x_ref, *rest):
        w_refs, keep_ref, o_ref = rest[:3], rest[3], rest[-1]
        begin = pl.program_id(0) * chunk
        value = 0.0
        for a in range(3):
            rows = pl.ds(pl.multiple_of(begin + a * width, width), chunk)
            term = 0.0
            for j in range(3):
                term = term + lax.dot_general(
                    x_ref[rows, j * mid : (j + 1) * mid],
                    w_refs[2 - a][j],
                    contract_last,
                    preferred_element_type=f32,
                )
            value = value + (term if a == 1 else keep_ref[a] * term)
        o_ref[...] = value.astype(bf16)

    extra = [] if marker is None else [marker]
    once = pl.Buffered(1)
    one = pl.BlockSpec((3, block, mid), lambda c: (0, 0, 0), pipeline_mode=once)
    return pl.pallas_call(
        body,
        grid=(cells // chunk,),
        in_specs=[
            pl.BlockSpec((ext, deep), lambda c: (0, 0), pipeline_mode=once),
            one, one, one,
            pl.BlockSpec((3, chunk, 1), lambda c: (0, c, 0)),
        ]
        + [pl.BlockSpec(memory_space=pl.ANY)] * len(extra),
        out_specs=pl.BlockSpec((chunk, block), lambda c: (c, 0)),
        out_shape=jax.ShapeDtypeStruct((cells, block), bf16),
        compiler_params=pltpu.CompilerParams(vmem_limit_bytes=32 << 20),
        cost_estimate=small_cost,
    )(wide, *weight, keeps, *extra)


def weight_sums(sides, own, others, width, marker=None):
    _, cells, block = sides.shape
    mid = own.shape[1] // 3
    strips = 1 + len(others)
    strip = cells // strips

    if cells * mid > 3072 * 512:
        parts = [own[width : width + strip], *others]
        return jnp.stack(
            [
                sum(
                    dot(
                        sides[a, k * strip : (k + 1) * strip],
                        parts[k][:, j * mid : (j + 1) * mid],
                        contract_first,
                    )
                    for k in range(strips)
                ).astype(bf16)
                for a in range(3)
                for j in range(3)
            ]
        )

    def body(side_ref, own_ref, *rest):
        o_ref = rest[-1]
        terms = 0.0
        for k in range(strips):
            part = own_ref[width : width + strip, :] if k == 0 else rest[k - 1][...]
            terms = terms + lax.dot_general(
                side_ref[0, k * strip : (k + 1) * strip, :],
                part,
                contract_first,
                preferred_element_type=f32,
            )
        for j in range(3):
            o_ref[j] = terms[:, j * mid : (j + 1) * mid].astype(bf16)

    once = pl.Buffered(1)
    extra = [] if marker is None else [marker]
    return pl.pallas_call(
        body,
        grid=(3,),
        in_specs=[
            pl.BlockSpec((1, cells, block), lambda a: (a, 0, 0)),
            pl.BlockSpec(own.shape, lambda a: (0, 0), pipeline_mode=once),
        ]
        + [pl.BlockSpec((strip, 3 * mid), lambda a: (0, 0), pipeline_mode=once)] * len(others)
        + [pl.BlockSpec(memory_space=pl.ANY)] * len(extra),
        out_specs=pl.BlockSpec((3, block, mid), lambda a: (a, 0, 0)),
        out_shape=jax.ShapeDtypeStruct((9, block, mid), bf16),
        compiler_params=pltpu.CompilerParams(vmem_limit_bytes=44 << 20),
        cost_estimate=small_cost,
    )(sides, own, *others, *extra)


def pool_back(grads, projections, limits, shares, pooled, joined):
    scales, wide, deep = projections.shape
    cells, bins = pooled.shape
    _, more = grads.shape
    block = wide // 4

    def body(grad_ref, w_ref, share_ref, pool_ref, join_ref, o_ref):
        lane = lax.broadcasted_iota(jnp.int32, (deep, more), 1)
        grad = grad_ref[...].astype(f32)
        total = 0.0
        for s in range(scales):
            inside = (lane >= limits[s]) & (lane < limits[s + 1])
            part = jnp.where(inside, grad, 0.0).astype(bf16)
            total = total + jnp.dot(w_ref[s], part, preferred_element_type=f32)
        value = (total[:, :bins] * share_ref[...]).astype(bf16)
        o_ref[...] = join_ref[...].astype(f32) + lax.dot_general(
            pool_ref[...], value, contract_last, preferred_element_type=f32
        )

    return pl.pallas_call(
        body,
        grid=(4,),
        in_specs=[
            pl.BlockSpec((deep, more), lambda c: (0, 0)),
            pl.BlockSpec((scales, block, deep), lambda c: (0, c, 0)),
            pl.BlockSpec((1, bins), lambda c: (0, 0)),
            pl.BlockSpec((cells, bins), lambda c: (0, 0)),
            pl.BlockSpec((cells, block), lambda c: (0, c)),
        ],
        out_specs=pl.BlockSpec((cells, block), lambda c: (0, c)),
        out_shape=jax.ShapeDtypeStruct((cells, wide), f32),
        compiler_params=pltpu.CompilerParams(vmem_limit_bytes=40 << 20),
        cost_estimate=small_cost,
    )(grads, projections, shares, pooled, joined)


def silu_slope(value):
    sigmoid_value = jax.nn.sigmoid(value)
    return sigmoid_value * (1.0 + value * (1.0 - sigmoid_value))


def choose(options, index):
    value = options[0]
    for k in range(1, len(options)):
        value = jnp.where(index == k, options[k], value)
    return value


def table_at(values, index):
    return choose([jnp.int32(value) for value in values], index)


def tie(*arrays):
    return list(lax.optimization_barrier(tuple(arrays)))


class Rows:
    def __init__(self, own):
        self.count = lax.axis_size("row")
        self.row = lax.axis_index("row")
        self.right = self.left = own
        self.arrived = {}
        self.step = 0

    def kinds(self, k):
        return [(abs(z - (z ^ k)), int((z ^ k) > z)) for z in range(self.count)]

    def more(self):
        return self.step < self.count - 1

    def send(self):
        self.step += 1
        step, count = self.step, self.count
        to_right = [(z, z + 1) for z in range(step - 1, count - 1)]
        to_left = [(z, z - 1) for z in range(1, count - step + 1)]
        return [
            lax.ppermute(self.right, "row", to_right),
            lax.ppermute(self.left, "row", to_left),
        ]

    def receive(self, results):
        self.right, self.left = results[0], results[-1]
        self.arrived[self.step] = (self.right, self.left)

    def ready(self, k):
        return max(step for step, _ in self.kinds(k)) <= self.step

    def slot(self, k):
        each = self.kinds(k)
        options = sorted(set(each))
        which = table_at([options.index(kind) for kind in each], self.row)
        return choose([self.arrived[step][side] for step, side in options], which)


def place_images(pieces, kind=bf16):
    me = lax.axis_index("img")
    first = pieces[0]
    width = first.shape[1]
    shape = (first.shape[0], len(pieces) * width) + first.shape[2:]
    joined = jnp.zeros(shape, kind)
    for step, piece in enumerate(pieces):
        joined = lax.dynamic_update_slice_in_dim(
            joined, piece.astype(kind), (me ^ step) * width, 1
        )
    return joined


class Chain:
    def __init__(self, value, axes):
        self.value = value
        self.todo = []
        for axis in axes:
            step = 1
            while step < lax.axis_size(axis):
                self.todo.append((axis, step))
                step *= 2

    def send(self):
        return [swap(self.value, *self.todo[0])] if self.todo else []

    def receive(self, got):
        if got:
            self.value = self.value + got[0]
            self.todo = self.todo[1:]


def mark(*arrays):
    tiny = jnp.zeros((8, 128), f32)
    *arrays, tiny = tie(*arrays, tiny)
    return arrays, swap(tiny, "col", 1)


def add_low(a, b):
    return (a.astype(f32) + b.astype(f32)).astype(bf16)


class ImageSum:
    def __init__(self, x):
        self.x = x
        self.me = lax.axis_index("img")
        self.half = x.shape[1] // 8

    def piece(self, j, side):
        at = (self.me ^ j) * 2 * self.half + side * self.half
        return lax.dynamic_slice_in_dim(self.x, at, self.half, 1)

    def first_sends(self):
        return [
            jnp.concatenate([self.piece(1, 0), self.piece(3, 0)], axis=1),
            jnp.concatenate([self.piece(2, 1), self.piece(3, 1)], axis=1),
        ]

    def first(self, sends):
        return [swap(sends[0], "img", 1), swap(sends[1], "img", 2)]

    def second_sends(self, got):
        half = self.half
        self.own = [add_low(self.piece(0, k), got[k][:, :half]) for k in range(2)]
        return [
            add_low(self.piece(2, 0), got[0][:, half:]),
            add_low(self.piece(1, 1), got[1][:, half:]),
        ]

    def second(self, sends):
        return [swap(sends[0], "img", 2), swap(sends[1], "img", 1)]

    def reduced(self, got):
        self.own = [add_low(a, b) for a, b in zip(self.own, got)]
        return self.own

    def third(self, own):
        self.own = own
        return [swap(own[0], "img", 1), swap(own[1], "img", 2)]

    def fourth_sends(self, got):
        self.next = got
        return [jnp.concatenate([own, near], axis=1) for own, near in zip(self.own, got)]

    def fourth(self, sends):
        return [swap(sends[0], "img", 2), swap(sends[1], "img", 1)]

    def gathered(self, got):
        half = self.half
        own, near = self.own, self.next
        parts = [
            (0, 0, own[0]),
            (0, 1, own[1]),
            (1, 0, near[0]),
            (2, 1, near[1]),
            (2, 0, got[0][:, :half]),
            (3, 0, got[0][:, half:]),
            (1, 1, got[1][:, :half]),
            (3, 1, got[1][:, half:]),
        ]
        taps, _, mid = self.x.shape
        whole = jnp.zeros((taps, 8 * half, mid), f32)
        for j, side, part in parts:
            at = (self.me ^ j) * 2 * half + side * half
            whole = lax.dynamic_update_slice_in_dim(whole, part.astype(f32), at, 1)
        return whole


def join_cols(mine, others, axis):
    col = lax.axis_index("col")
    pieces = [mine] + list(others)
    return jnp.concatenate([choose(pieces, col ^ c) for c in range(len(pieces))], axis=axis)


def row_halo(lines):
    count = lax.axis_size("row")
    above = lax.ppermute(lines[-1:], "row", [(i, i + 1) for i in range(count - 1)])
    below = lax.ppermute(lines[:1], "row", [(i + 1, i) for i in range(count - 1)])
    return jnp.concatenate([above, lines, below], axis=0)


def on_device(
    features,
    region_boxes,
    labels,
    branch_projection_weight,
    branch_gain,
    branch_bias,
    conv_w,
    conv_gain,
    conv_bias,
    class_w,
    class_bias,
):
    _, tile_h, tile_w, channels_in = features.shape
    pixels = tile_h * tile_w
    images, row_count, col_count = (lax.axis_size(axis) for axis in ("img", "row", "col"))
    img, row, col = (lax.axis_index(axis) for axis in ("img", "row", "col"))
    groups = row_count * col_count
    block, taps, mid = conv_w.shape
    branch_width = branch_projection_weight.shape[2]
    feature_rows = channels_in // (block * col_count)
    regions = region_boxes.shape[1]
    height, width = row_count * tile_h, col_count * tile_w
    all_cells = images * height * width
    canvas_box = region_boxes[0]
    table = bin_constants(regions)
    bins = table.shape[0]
    limits = [0]
    for scale in bin_scales:
        limits.append(limits[-1] + regions * scale * scale)
    scale_rows = [
        jnp.asarray((table[:, 0] == position).astype(np.float32)) for position in range(4)
    ]

    weight = jnp.transpose(conv_w, (1, 0, 2))
    share = block // images
    own_share, tile = tie(
        lax.dynamic_slice_in_dim(weight, img * share, share, 1),
        features[0].reshape(pixels, channels_in),
    )
    rows = Rows(own_share)

    def by_line(nine):
        return [nine[3 * a : 3 * a + 3] for a in range(3)]

    weights = [by_line(weight)]
    waiting = {"next": 1, "send": [], "plan": [], "slot": None, "place": []}

    def weight_plan(before=()):
        plan, send = [], [[], []]
        if waiting["slot"] is not None:
            pieces = waiting["slot"]
            half = share // 2
            send[0].append(pieces[2][:, half:])
            send[1].append(pieces[1][:, :half])
            plan.append(("close", pieces))
        if waiting["next"] < row_count and rows.ready(waiting["next"]):
            part = rows.slot(waiting["next"])
            waiting["next"] += 1
            send[0].append(part)
            send[1].append(part)
            plan.append(("cross", part))
        send = [jnp.concatenate(arrays, axis=1) for arrays in send if arrays]
        placed = waiting["place"] if plan else []
        got, waiting["mark"] = mark(*send, *before, *placed)
        waiting["send"], waiting["plan"] = got[: len(send)], plan
        end = len(got) - len(placed)
        place_now(got[end:] if plan else waiting["place"])
        return got[len(send) : end]

    def lines_of(pieces):
        return [place_images([piece[3 * a : 3 * a + 3] for piece in pieces]) for a in range(3)]

    def place_now(pieces):
        if pieces:
            weights.append(lines_of(pieces))
        waiting["place"] = []

    def weight_phase(more=(), hold=()):
        flights = [swap(send, "img", k + 1) for k, send in enumerate(waiting["send"])]
        count = len(flights)
        hop = waiting["hop"]
        flights += hop
        got = tie(*flights, *more, *hold)
        if hop:
            rows.receive(got[count : len(flights)])
        waiting["hop"] = rows.send() if rows.more() else []
        waiting["slot"] = None
        at = 0
        for what, kept in waiting["plan"]:
            size = share // 2 if what == "close" else share
            part = [array[:, at : at + size] for array in got[:count]]
            at += size
            if what == "close":
                far = jnp.concatenate([part[1], part[0]], axis=1)
                waiting["place"] = kept + [far]
            else:
                waiting["slot"] = [kept] + part
        at = len(flights)
        return got[at : at + len(more)], got[at + len(more) :]

    waiting["hop"] = rows.send()

    tile_ext = row_halo(tile.reshape(tile_h, tile_w, channels_in))

    def channels_of(c):
        at = [(r * col_count + c) * block for r in range(feature_rows)]
        return jnp.stack([tile_ext[..., k : k + block] for k in at])

    by_col = [channels_of(c) for c in range(col_count)]
    sent = [choose(by_col, col ^ step) for step in range(col_count)]
    strip_ext = join_cols(
        sent[0], [swap(sent[step], "col", step) for step in range(1, col_count)], 2
    )
    weight_phase()
    (strip_ext,) = weight_plan([strip_ext])

    boxes = of_bin_boxes(canvas_box, table)
    scale, bin_i, bin_j = (jnp.asarray(table[:, k]) for k in (1, 3, 4))
    extent_y, extent_x = boxes[:, 2] - boxes[:, 0], boxes[:, 3] - boxes[:, 1]
    edges = (
        boxes[:, 0] + lax.div(bin_i * extent_y, scale),
        boxes[:, 0] + lax.div((bin_i + 1) * extent_y + scale - 1, scale),
        boxes[:, 1] + lax.div(bin_j * extent_x, scale),
        boxes[:, 1] + lax.div((bin_j + 1) * extent_x + scale - 1, scale),
    )
    sizes = ((edges[1] - edges[0]) * (edges[3] - edges[2])).astype(f32)
    top, left = row * tile_h, col * tile_w
    tile_y, tile_x = grid_cells(
        top + jnp.arange(tile_h, dtype=jnp.int32), left + jnp.arange(tile_w, dtype=jnp.int32)
    )
    pooling = members(edges, tile_y, tile_x)
    local_means = dot(pooling, tile) / sizes[:, None]
    local_low = local_means.astype(bf16)
    pre_local = jnp.concatenate(
        [
            dot(
                branch_projection_weight[position],
                local_low[limits[position] : limits[position + 1]],
                (((0,), (1,)), ((), ())),
            )
            for position in range(4)
        ],
        axis=1,
    )
    pre = lax.psum_scatter(pre_local, ("row", "col"), scatter_dimension=0, tiled=True)
    cat_blocks = strip_ext.reshape(feature_rows, -1, block)
    slots_of = row ^ jnp.arange(row_count, dtype=jnp.int32)
    cat_wide = shifted(
        cat_blocks, canvas_box, top - 1, width, places=slots_of[:feature_rows],
        out_blocks=row_count,
    )
    _, (pre, cat_wide) = weight_phase(hold=[pre, cat_wide])
    part = branch_width // groups
    group = row * col_count + col

    def by_scale(value):
        return jnp.stack([jnp.sum(value * line[None], axis=1) for line in scale_rows])

    def to_bins(value):
        return sum(value[k][:, None] * scale_rows[k][None] for k in range(4))

    def branch_part(value):
        return to_bins(lax.dynamic_slice_in_dim(value, group * part, part, 1))

    counts = np.asarray([images * regions * s * s for s in bin_scales], np.float32)[:, None]
    moments = butterfly(jnp.concatenate([by_scale(pre), by_scale(pre * pre)], axis=0), ("img",))
    moments, cat_wide = weight_plan([moments, cat_wide])
    center = moments[:4] / counts
    inverse = lax.rsqrt(moments[4:] / counts - center * center + norm_eps)
    gain_part = branch_part(branch_gain)
    inverse_bins = to_bins(inverse)
    normed = (pre - to_bins(center)) * inverse_bins
    before = gain_part * normed + branch_part(branch_bias)
    act_branch = lax.all_gather(
        (jax.nn.silu(before) + waiting["mark"][0, 0]).astype(bf16),
        ("row", "col"), axis=0, tiled=True,
    )

    def block_rows_of(r):
        first = (r * col_count + col) * block - channels_in
        position = lax.div(first, branch_width)
        taken = lax.dynamic_slice_in_dim(
            act_branch, jnp.maximum(lax.rem(first, branch_width), 0), block, 0
        )
        keep = jnp.asarray(table[:, 0]) == position
        return jnp.where(keep[None], taken, jnp.zeros((), bf16)), keep

    strip_cols = jnp.arange(width, dtype=jnp.int32)
    strip_cells = tile_h * width
    ext_cells = strip_cells + 2 * width

    def ext_spread(source):
        lines = source * tile_h - 1 + jnp.arange(tile_h + 2, dtype=jnp.int32)
        return spreads(boxes, table, *grid_cells(lines, strip_cols))

    def up_blocks(spread, r):
        return dot(spread, block_rows_of(r)[0], (((0,), (1,)), ((), ()))).astype(bf16)

    spread_ext = ext_spread(row)
    ups = jnp.stack([up_blocks(spread_ext, r) for r in range(feature_rows, row_count)])
    cat_wide = shifted(
        ups, canvas_box, top - 1, width, places=slots_of[feature_rows:],
        out_blocks=row_count, into=cat_wide,
    )
    upper, lower = row_masks(canvas_box, jnp.arange(height, dtype=jnp.int32), strip_cols)

    def strip_of(cells, source):
        return lax.dynamic_slice_in_dim(cells, source * strip_cells, strip_cells, 0)

    keeps = jnp.stack(
        [strip_of(upper, row), jnp.ones((strip_cells,), bool), strip_of(lower, row)]
    ).astype(f32)[:, :, None]

    depth = row_count // 2
    place = lax.rem(row, depth)
    _, (cat_wide, cat_blocks) = weight_phase(hold=[cat_wide, cat_blocks])

    def moved(step):
        return lax.dynamic_index_in_dim(cat_blocks, place ^ step, 0, keepdims=False)

    own_ext, *sends, cat_wide = weight_plan([moved(step) for step in range(depth)] + [cat_wide])
    feature_exts = {0: own_ext}
    hidden_strip = conv_slot(cat_wide, 0, weights[0], keeps, None, width)
    for slot in range(1, row_count):
        while len(weights) <= slot:
            step = len(feature_exts)
            more = [swap(sends[step - 1], "row", step)] if step < depth else []
            got, hold = weight_phase(more=more, hold=[hidden_strip])
            if got:
                feature_exts[step] = got[0]
            if len(weights) == row_count - 2:
                hidden_strip, mean_moves = weight_plan(hold + [local_means.astype(bf16)])
            else:
                (hidden_strip,) = weight_plan(hold)
        hidden_strip = conv_slot(cat_wide, slot, weights[slot], keeps, hidden_strip, width)
    for step in range(1, depth):
        if step not in feature_exts:
            feature_exts[step] = swap(sends[step - 1], "row", step)
    own_means = lax.psum_scatter(mean_moves, ("row", "col"), scatter_dimension=1, tiled=True)
    hidden_strip = hidden_strip.reshape(tile_h, width, mid)

    def cells_of(step):
        return lax.dynamic_slice_in_dim(hidden_strip, (col ^ step) * tile_w, tile_w, 1)

    hidden = cells_of(0)
    for step in range(1, col_count):
        hidden = hidden + swap(cells_of(step), "col", step)
    hidden = hidden.reshape(pixels, mid)

    everywhere = ("col", "img", "row")
    mid_moments = butterfly(
        jnp.stack([jnp.sum(hidden, axis=0), jnp.sum(hidden * hidden, axis=0)]), everywhere
    )
    center_mid = mid_moments[0] / all_cells
    inverse_mid = lax.rsqrt(mid_moments[1] / all_cells - center_mid * center_mid + norm_eps)
    normed_mid = (hidden - center_mid) * inverse_mid
    before_mid = conv_gain * normed_mid + conv_bias
    act_mid = jax.nn.silu(before_mid).astype(bf16)
    logits = dot(act_mid, class_w) + class_bias
    classes = class_w.shape[1]
    onehot = (
        labels[0].reshape(pixels)[:, None] == jnp.arange(classes, dtype=jnp.int32)[None, :]
    ).astype(f32)
    grad_logits = (jax.nn.softmax(logits, axis=-1) - onehot).astype(bf16)
    grad_before = dot(grad_logits, class_w, contract_last) * silu_slope(before_mid)
    mid_grads = butterfly(
        jnp.stack([jnp.sum(grad_before * normed_mid, axis=0), jnp.sum(grad_before, axis=0)]),
        everywhere,
    )
    low_zero = jnp.zeros((), bf16)
    lower_half = row < depth
    up_exts = [choose([ups[r] for r in range(depth)], place)] + [
        up_blocks(ext_spread(row ^ step), feature_rows + place) for step in range(1, depth)
    ]
    exts = [
        (
            jnp.where(lower_half, up_exts[step], feature_exts[step]),
            jnp.where(lower_half, feature_exts[step], up_exts[step]),
        )
        for step in range(depth)
    ]
    sides = []
    for kind in range(2):
        lines = []
        for a in range(3):
            pieces = []
            for step in range(depth):
                piece = exts[step][kind][a * width : a * width + strip_cells]
                if a != 1:
                    keep = strip_of((upper, None, lower)[a], row ^ step)
                    piece = jnp.where(keep[:, None], piece, low_zero)
                pieces.append(piece)
            lines.append(jnp.concatenate(pieces, axis=0))
        sides.append(lines)

    mid_grads, home_side, away_side = tie(mid_grads, jnp.stack(sides[1]), jnp.stack(sides[0]))
    conv_gain_grad, conv_bias_grad = mid_grads[0], mid_grads[1]
    background = ("img", "row", "col")
    class_chain = Chain(
        jnp.concatenate(
            [
                dot(act_mid, grad_logits, contract_first),
                jnp.sum(grad_logits.astype(f32), axis=0, keepdims=True),
            ],
            axis=0,
        ),
        background,
    )
    grad_hidden = (
        conv_gain
        * inverse_mid
        * (grad_before - conv_bias_grad / all_cells - normed_mid * conv_gain_grad / all_cells)
    ).astype(bf16)

    def pair_strip(mine):
        return [swap(mine, "col", step) for step in range(1, col_count)]

    grad_tile = grad_hidden.reshape(tile_h, tile_w, mid)
    hops = [swap(grad_tile, "row", step) for step in range(1, depth)]
    grad_ext = row_halo(grad_tile)
    grad_ext = join_cols(grad_ext, pair_strip(grad_ext), 1)
    grad_strip = grad_ext[1:-1]
    grad_ext = grad_ext.reshape(1, ext_cells, mid)
    own_wide = shifted(grad_ext, canvas_box, top - 1, width, reverse=True)[0]

    def input_grads(slot, marker=None):
        return grad_slot(own_wide, weights[slot], keeps, width, marker)

    def phase(flights, hold=(), chain=True):
        sent = class_chain.send() if chain else []
        got = tie(*flights, *sent, *hold)
        class_chain.receive(got[len(flights) : len(flights) + len(sent)])
        return got[: len(flights)], got[len(flights) + len(sent) :]

    held = [input_grads(slot) for slot in range(depth)]
    hops += [swap(own_means, "img", 1), swap(own_means, "img", 2)]
    hops, cat_grads = phase(hops, held)
    *hops, means_one, means_two = hops
    cat_grads = list(cat_grads)
    others = []
    for k, tile_there in enumerate(hops):
        strip = join_cols(tile_there, pair_strip(tile_there), 1)
        others.append(
            shifted(
                strip.reshape(1, strip_cells, mid), canvas_box, (row ^ (k + 1)) * tile_h, width,
                reverse=True,
            )[0]
        )
    class_sent = class_chain.send()
    away = ImageSum(weight_sums(away_side, own_wide, others, width))
    (*sends, class_got), marker = mark(*away.first_sends(), *class_sent)
    class_chain.receive([class_got])
    flights = away.first(sends)
    flights.append(swap(means_one, "img", 2))
    home = weight_sums(home_side, own_wide, others, width, marker)
    got, (home,) = phase(flights, [home])
    home = ImageSum(home)
    means = [own_means, means_one, means_two, got.pop()]
    sends, marker = mark(*away.second_sends(got))
    flights = away.second(sends)
    held = [input_grads(slot, marker) for slot in range(depth, row_count)]
    got, held = phase(flights, held)
    cat_grads += held
    *sends, far_own, far_next = tie(*home.first_sends(), *away.reduced(got))
    logits_out = logits.reshape(1, tile_h, tile_w, classes)
    got, (far_next, logits_out, *means) = phase(
        home.first(sends) + [swap(far_own, "row", depth)], [far_next, logits_out, *means]
    )
    crossed = [got.pop()]
    sends, second_mark = mark(*home.second_sends(got))
    flights = home.second(sends) + [swap(far_next, "row", depth)]
    by_row = [choose(cat_grads, row ^ r) for r in range(row_count)]
    spread_strip = lax.slice_in_dim(spread_ext, width, width + strip_cells, axis=1)
    grad_bins_local = jnp.zeros((branch_width, bins), f32)
    for r in range(feature_rows, row_count):
        first = (r * col_count + col) * block - channels_in
        keep = jnp.asarray(table[:, 0]) == lax.div(first, branch_width)
        terms = dot(by_row[r], spread_strip, (((0,), (1,)), ((), ())))
        terms = jnp.where(keep[None], terms, 0.0)
        at = lax.rem(first, branch_width)
        old = lax.dynamic_slice_in_dim(grad_bins_local, at, block, 0)
        grad_bins_local = lax.dynamic_update_slice_in_dim(grad_bins_local, old + terms, at, 0)
    grad_bins = lax.psum_scatter(
        grad_bins_local.astype(bf16), ("row", "col"), scatter_dimension=0, tiled=True
    ).astype(f32)
    grad_act = (grad_bins + second_mark[0, 0]) * silu_slope(before)
    branch_sums = butterfly(
        jnp.concatenate([by_scale(grad_act * normed), by_scale(grad_act)], axis=0), ("img",)
    )
    grad_pre = (
        gain_part
        * inverse_bins
        * (
            grad_act
            - to_bins(branch_sums[4:] / counts)
            - normed * to_bins(branch_sums[:4] / counts)
        )
    ).astype(bf16)
    own_features = [
        by_row[r].reshape(tile_h, width, block) for r in range(feature_rows)
    ]

    def feature_grads_of(step):
        return jnp.stack(
            [
                choose(
                    [one[:, c * tile_w : (c + 1) * tile_w] for c in range(col_count)], col ^ step
                ).reshape(pixels, block)
                for one in own_features
            ]
        )

    by_step = [feature_grads_of(0)] + [
        swap(feature_grads_of(step), "col", step) for step in range(1, col_count)
    ]
    by_block = [choose(by_step, col ^ c) for c in range(col_count)]
    joined = jnp.concatenate(
        [by_block[c][r] for r in range(feature_rows) for c in range(col_count)], axis=1
    )
    by_scales = jnp.asarray(table[:, 0][None, :] == np.arange(4)[:, None], bf16)
    means = [
        jnp.concatenate([part * line[:, None] for line in by_scales], axis=1) for part in means
    ]
    sums = branch_sums.T
    high = sums.astype(bf16)
    middle = (sums - high.astype(f32)).astype(bf16)
    low = (sums - high.astype(f32) - middle.astype(f32)).astype(bf16)
    piece = jnp.concatenate([grad_pre, high, middle, low], axis=1)
    flights += [swap(piece, "img", 1), swap(piece, "img", 2)]
    pooled = jnp.transpose(pooling)
    got, (joined, pooled, *means) = phase(flights, [joined, pooled, *means], chain=False)
    *got, piece_one, piece_two = got
    home_own = home.reduced(got[:2])
    crossed.append(got[2])
    home_own = [add_low(a, b) for a, b in zip(home_own, crossed)]
    got, _ = phase(home.third(home_own) + [swap(piece_one, "img", 2)])
    packed = jnp.stack([piece, piece_one, piece_two, got.pop()])
    sends = home.fourth_sends(got)
    sends, fourth_mark = mark(*sends, *home.own, *home.next)
    home.own, home.next = sends[2:4], sends[4:]
    got = home.fourth(sends)
    while class_chain.todo:
        phase([])
    class_w_grad, class_bias_grad = class_chain.value[:mid], class_chain.value[mid]
    gathered = lax.all_gather(
        packed + fourth_mark[0, 0].astype(bf16), ("row", "col"), axis=1, tiled=True
    )
    ends = gathered[0, :, bins:].astype(f32)
    branch_all = (ends[:, :8] + ends[:, 8:16] + ends[:, 16:]).T
    branch_gain_grad, branch_bias_grad = branch_all[:4], branch_all[4:]
    branch_w_grad = sum(
        dot(means[k], gathered[k, :, :bins], (((0,), (1,)), ((), ()))) for k in range(images)
    ).reshape(4, -1, branch_width)
    feature_grad = pool_back(
        gathered[0], branch_projection_weight, limits, 1.0 / sizes[None], pooled, joined
    ).reshape(1, tile_h, tile_w, channels_in)
    feature_grad, branch_w_grad, *got = tie(feature_grad, branch_w_grad, *got)
    conv_w_grad = home.gathered(got)
    conv_w_grad = jnp.transpose(conv_w_grad, (1, 0, 2))
    return (
        logits_out,
        feature_grad,
        branch_w_grad,
        branch_gain_grad,
        branch_bias_grad,
        conv_w_grad,
        conv_gain_grad,
        conv_bias_grad,
        class_w_grad,
        class_bias_grad,
    )


def solution(mesh):
    return jax.shard_map(
        on_device,
        mesh=mesh,
        in_specs=(
            P("img", "row", "col", None),
            P("img", None, None),
            P("img", "row", "col"),
            P(),
            P(),
            P(),
            P(("row", "col"), None, None),
            P(),
            P(),
            P(),
            P(),
        ),
        out_specs=(
            P("img", "row", "col", None),
            P("img", "row", "col", None),
            P(None, ("row", "col"), None),
            P(),
            P(),
            P(("row", "col"), None, None),
            P(),
            P(),
            P(),
            P(),
        ),
        check_vma=False,
    )
```
